32 devices in a mesh: leaf: 16 (over z, y, core), grp: 2 (over x).
Axes of the slice: x: 2, y: 2, z: 4, core: 2. Of those that a mesh axis runs over, the one named last changes fastest.
Arguments:
- slot_parent: int32 [32], P(('leaf', 'grp')), may hold values from -1 to 7, as said below
- leaf_matrix: float32 [32, 384, 384], P(('leaf', 'grp')), as said below
- coupling: float32 [32, 384, 128], P(('leaf', 'grp')), may hold values from -0.3125 to 0.3125
- leaf_residual_rows: float32 [32, 384], P(('leaf', 'grp')), may hold values from -6 to 6
- node_matrix: float32 [16, 128, 128], P('grp', 'leaf'), as said below
- node_link: float32 [16, 128, 128], P('grp', 'leaf'), may hold values from -0.5 to 0.5
- node_rhs: float32 [16, 128], P('grp', 'leaf'), may hold values from -6 to 6
- root_matrix: float32 [128, 128], replicated, as said below
- root_rhs: float32 [128], replicated, may hold values from -6 to 6
Outputs:
- leaf_dir: float32 [32, 384], P(('leaf', 'grp'))
- node_dir: float32 [16, 128], P('grp', 'leaf')
- root_dir: float32 [128], replicated
The draws below stay inside these ranges and needn't reach their ends.
Inputs may be any that keep to these rules, and one draw needn't show every extreme that they name: `slot_parent`: -1 marks an empty slot; otherwise the value is the section-2 node, among the 8 nodes of the slot's grp index, to which the leaf belongs. On every device the live slots come first; a device may hold no live slot or only live slots. `leaf_matrix`: each block is symmetric positive definite with smallest eigenvalue at least 0.1. `node_matrix`: each block is symmetric positive definite with smallest eigenvalue at least 0.1. `root_matrix`: symmetric positive definite with smallest eigenvalue at least 0.1.
All inputs are finite; a program needn't handle non-finite values.
Results may differ from the reference program's by a relative error of at most 0.00018.
Values sent between devices are 32-bit elements; how exact they have to be, the bound alone decides.
No kernel may reach another device: no remote copies, remote signals or barrier semaphores. Data moves between devices by JAX's collectives and lax.ppermute only.
A program may use at most 64 MiB of HBM per device.

```python
import math
import jax
import jax.numpy as jnp
from jax import lax

LEAF_ROWS = 384
LINK_WIDTH = 128
R = 128
GROUP_NODES = 8
DEVICE_SLOTS = 1
TOTAL_SLOTS = 32
NODES = 16
N_GRP = 2


def positive_definite_blocks(base_key, block_count, matrix_order):
    block_keys = jax.random.split(base_key, block_count)

    def one_block(block_key):
        entry_key, margin_key = jax.random.split(block_key)
        factor = jax.random.normal(entry_key, (matrix_order, matrix_order), jnp.float32)
        margin = jnp.exp(jax.random.uniform(margin_key, (matrix_order,), jnp.float32, math.log(0.1), math.log(3.0)))
        product = jnp.dot(factor, factor.T, precision=lax.Precision.HIGHEST)
        product = (product + product.T) * (0.5 / matrix_order)
        identity = jnp.eye(matrix_order, dtype=jnp.float32)
        return product + identity * margin[:, None]
    return lax.map(one_block, block_keys)


def draw_leaf_matrix(key, part):
    return positive_definite_blocks(jax.random.fold_in(key, 11), TOTAL_SLOTS, LEAF_ROWS)


def draw_node_matrix(key, part):
    return positive_definite_blocks(jax.random.fold_in(key, 12), NODES, LINK_WIDTH)


def draw_root_matrix(key, part):
    return positive_definite_blocks(jax.random.fold_in(key, 13), 1, R)[0]


def draw_slot_parent(key, part):
    base_key = jax.random.fold_in(key, 14)
    count_key, parent_random_key = jax.random.split(base_key)
    device_list = TOTAL_SLOTS // DEVICE_SLOTS
    active_count = jax.random.randint(count_key, (device_list,), 0, DEVICE_SLOTS + 1)
    active_count = active_count.at[0].set(0).at[device_list - 1].set(DEVICE_SLOTS)
    parent_nodes = jax.random.randint(parent_random_key, (TOTAL_SLOTS,), 0, GROUP_NODES)
    parent_nodes = parent_nodes.at[TOTAL_SLOTS - 1].set(GROUP_NODES - 1)
    slot_position = jnp.arange(TOTAL_SLOTS, dtype=jnp.int32) % DEVICE_SLOTS
    owning_index = jnp.arange(TOTAL_SLOTS, dtype=jnp.int32) // DEVICE_SLOTS
    return jnp.where(slot_position < active_count[owning_index], parent_nodes, -1).astype(jnp.int32)


def levels(key, dims, cuts, low, largest):
    gain = 1.0
    for dim, parts in cuts:
        heights = jax.random.uniform(jax.random.fold_in(jax.random.fold_in(key, 6), dim), (parts,), jnp.float32, low / len(cuts), largest / len(cuts))
        gain = gain * jnp.repeat(jnp.exp(heights), dims[dim] // parts).reshape((-1,) + (1,) * (len(dims) - 1 - dim))
    return gain


def noise(key, extent, scale, limit, pieces=(), kind=jnp.bfloat16):
    drawn = scale * jax.random.normal(key, extent, jnp.float32)
    if pieces:
        drawn = drawn * levels(key, extent, pieces, -0.22, 0.18)
    return jnp.clip(drawn, -limit, limit).astype(kind)


def setup_inputs(seed: int = 0) -> dict:
    seeds = jax.random.split(jax.random.key(seed), 10)
    return {
        "slot_parent": draw_slot_parent(jax.random.fold_in(seeds[9], 71), 0),
        "leaf_matrix": draw_leaf_matrix(jax.random.fold_in(seeds[9], 71), 0),
        "coupling": noise(seeds[2], (TOTAL_SLOTS, LEAF_ROWS, LINK_WIDTH), LEAF_ROWS ** -0.5, 0.3125, ((0, 32),), jnp.float32),
        "leaf_residual_rows": noise(seeds[3], (TOTAL_SLOTS, LEAF_ROWS), 1.0, 6.0, ((0, 32),), jnp.float32),
        "node_matrix": draw_node_matrix(jax.random.fold_in(seeds[9], 71), 0),
        "node_link": noise(seeds[5], (NODES, LINK_WIDTH, R), LINK_WIDTH ** -0.5, 0.5, ((0, 2), (1, 16)), jnp.float32),
        "node_rhs": noise(seeds[6], (NODES, LINK_WIDTH), 1.0, 6.0, ((0, 2), (1, 16)), jnp.float32),
        "root_matrix": draw_root_matrix(jax.random.fold_in(seeds[9], 71), 0),
        "root_rhs": noise(seeds[8], (R,), 1.0, 6.0, (), jnp.float32),
    }


highest = lax.Precision.HIGHEST

def lower_solve(factor, values):
    return lax.linalg.triangular_solve(factor, values, left_side=True, lower=True)

def upper_solve(factor, values):
    return lax.linalg.triangular_solve(factor, values, left_side=True, lower=True, transpose_a=True)

def leaf_factor(matrix, cpl_block, rhs_block):
    factor = jnp.linalg.cholesky(matrix)
    solved = lower_solve(factor, cpl_block)
    reduced = lower_solve(factor, rhs_block[:, None])[:, 0]
    return (factor, solved, reduced)

def reference(slot_parent, leaf_matrix, coupling, leaf_residual_rows, node_matrix, node_link, node_rhs, root_matrix, root_rhs):
    slot_numbers = jnp.arange(TOTAL_SLOTS, dtype=jnp.int32)
    set_index = slot_numbers // DEVICE_SLOTS % N_GRP
    active = slot_parent >= 0
    target = jnp.where(active, set_index * GROUP_NODES + slot_parent, 0).astype(jnp.int32)
    weight = active.astype(jnp.float32)

    def accumulate(carry, item):
        matrix, cpl_block, rhs_block, node_index, live_weight = item
        factor, solved, reduced = leaf_factor(matrix, cpl_block, rhs_block)
        gram = jnp.dot(solved.T, solved, precision=highest)
        projected = jnp.dot(solved.T, reduced, precision=highest)
        sums, vectors = carry
        sums = sums.at[node_index].add(live_weight * gram)
        vectors = vectors.at[node_index].add(live_weight * projected)
        return ((sums, vectors), None)
    start = (jnp.zeros((NODES, LINK_WIDTH, LINK_WIDTH), jnp.float32), jnp.zeros((NODES, LINK_WIDTH), jnp.float32))
    (sums, vectors), unused = lax.scan(accumulate, start, (leaf_matrix, coupling, leaf_residual_rows, target, weight))
    schur = node_matrix + sums
    node_vec = vectors - node_rhs
    node_fac = jnp.linalg.cholesky(schur)
    link_solved = lower_solve(node_fac, node_link)
    vec_solved = lower_solve(node_fac, node_vec[:, :, None])[:, :, 0]
    root_sys = root_matrix + jnp.einsum('kar,kas->rs', link_solved, link_solved, precision=highest)
    root_vec = root_rhs - jnp.einsum('kar,ka->r', link_solved, vec_solved, precision=highest)
    root_fac = jnp.linalg.cholesky(root_sys)
    root_dir = upper_solve(root_fac, lower_solve(root_fac, root_vec[:, None]))[:, 0]
    moved = vec_solved + jnp.einsum('kar,r->ka', link_solved, root_dir, precision=highest)
    node_dir = upper_solve(node_fac, moved[:, :, None])[:, :, 0]

    def leaf_solve(item):
        matrix, cpl_block, rhs_block, node_index, live_weight = item
        factor, solved, reduced = leaf_factor(matrix, cpl_block, rhs_block)
        parent_dir = node_dir[node_index]
        correction = reduced - jnp.dot(solved, parent_dir, precision=highest)
        return live_weight * upper_solve(factor, correction[:, None])[:, 0]
    leaf_dir = lax.map(leaf_solve, (leaf_matrix, coupling, leaf_residual_rows, target, weight))
    return (leaf_dir, node_dir, root_dir)
```

```python
import functools

import jax
import jax.numpy as jnp
from jax import lax
from jax.experimental import pallas as pl
from jax.experimental.pallas import tpu as pltpu
from jax.sharding import PartitionSpec as P

f32 = jnp.float32
bf16 = jnp.bfloat16
FLOOR = 0.1
COARSE = 0.15
MOST_STEPS = 24
ACCEPT = 4e-8


def mul(a, b):
    return jnp.dot(a, b, preferred_element_type=f32)


def nt(a, b):
    return lax.dot_general(a, b, (((1,), (1,)), ((), ())), preferred_element_type=f32)


def split(a):
    high = a.astype(bf16)
    return high, (a - high.astype(f32)).astype(bf16)


def split3(a):
    high = a.astype(bf16)
    rest = a - high.astype(f32)
    mid = rest.astype(bf16)
    return high, mid, (rest - mid.astype(f32)).astype(bf16)


def mul3(a, b):
    ah, al = split(a)
    bh, bl = split(b)
    return mul(ah, bh) + (mul(ah, bl) + mul(al, bh))


def nt3(a, b):
    ah, al = split(a)
    bh, bl = split(b)
    return nt(ah, bh) + (nt(ah, bl) + nt(al, bh))


def grid_of(rows, cols):
    return (
        lax.broadcasted_iota(jnp.int32, (rows, cols), 0),
        lax.broadcasted_iota(jnp.int32, (rows, cols), 1),
    )


def identity(n):
    row, col = grid_of(n, n)
    return (row == col).astype(f32)


def column_of(row_vector, n):
    return jnp.broadcast_to(row_vector, (128, n)).T


def pack_symmetric(full, extra):
    n = full.shape[0]
    half = n // 2
    row, col = grid_of(half, n)
    lower = full[half:]
    moved = pltpu.roll(lower, half, 1)
    top = jnp.where(col < row, moved, full[:half])
    diagonal = jnp.sum(jnp.where(col == row + half, lower, 0.0), axis=0, keepdims=True)
    row8, _ = grid_of(8, n)
    tail = jnp.where(row8 == 0, jnp.broadcast_to(extra, (8, n)), 0.0)
    tail = jnp.where(row8 == 1, jnp.broadcast_to(diagonal, (8, n)), tail)
    return top, tail


def unpack_symmetric(top, diagonal):
    half, n = top.shape
    row, col = grid_of(half, n)
    flipped = jnp.concatenate([top, jnp.zeros_like(top)], axis=0).T
    upper = jnp.where((col < half) & (col < row), flipped[:half], top)
    inner = pltpu.roll(jnp.where(col < row, top, flipped[:half]), half, 1)
    inner = jnp.where(col == row + half, jnp.broadcast_to(diagonal, (half, n)), inner)
    lower = jnp.where(col < half, flipped[half:], inner)
    return jnp.concatenate([upper, lower], axis=0)


def coarse_inverse(count, bound, matrix_of, high, inv):
    n = high.shape[1]
    delta = (bound - FLOOR) / (bound + FLOOR)
    alpha = 2.0 / (bound + FLOOR)
    scale = alpha * 2.0 / (2.0 - delta * delta)
    for i in range(count):
        inv[i] = (scale * (2.0 * identity(n) - alpha * matrix_of(i))).astype(bf16)

    def step(carry):
        delta, count_left = carry
        scale = 2.0 / (2.0 - delta * delta)
        for i in range(count):
            now = inv[i]
            error = (identity(n) - mul(high[i], now)).astype(bf16)
            inv[i] = (scale * (now.astype(f32) + mul(now, error))).astype(bf16)
        return delta * delta / (2.0 - delta * delta), count_left - 1

    start = (delta * delta / (2.0 - delta * delta), jnp.int32(MOST_STEPS))
    lax.while_loop(lambda c: (c[0] > COARSE) & (c[1] > 0), step, start)


def refine(matrix, inverse, right):
    high, mid, low = split3(matrix)
    step0 = mul(inverse, right.astype(bf16)).astype(bf16)
    rest = right - (mul(high, step0) + (mul(mid, step0) + mul(low, step0)))
    step1 = mul(inverse, rest.astype(bf16)).astype(bf16)
    rest = rest - (mul(high, step1) + mul(mid, step1))
    step2 = mul(inverse, rest.astype(bf16)).astype(bf16)
    rest = rest - (mul(high, step2) + mul(mid, step2))
    step3 = mul(inverse, rest.astype(bf16))
    return step0.astype(f32) + (step1.astype(f32) + (step2.astype(f32) + step3)), rest


def misfits(rest, right):
    got = jnp.sum(rest * rest, axis=0, keepdims=True)
    allowed = ACCEPT * jnp.sum(right * right, axis=0, keepdims=True)
    return jnp.where(got <= allowed, 0.0, 1.0)


def eliminate(work):
    n, width = work.shape

    def step(k, carry):
        row, col = grid_of(8, width)
        base = pl.multiple_of((k // 8) * 8, 8)
        block = work[pl.ds(base, 8), :]
        pivot_row = jnp.sum(jnp.where(row == k - base, block, 0.0), axis=0, keepdims=True)
        pivot = jnp.sum(jnp.where(col[:1] == k, pivot_row, 0.0), axis=1, keepdims=True)
        scaled = pivot_row / pivot
        full = work[...]
        row, col = grid_of(n, width)
        column = jnp.sum(jnp.where(col == k, full, 0.0), axis=1, keepdims=True)
        work[...] = jnp.where(row == k, scaled, full - column * scaled)
        return carry

    lax.fori_loop(0, n, step, 0)


def leaf_kernel(parent, matrix, coupling, residual, solved, message, high, inv, work):
    n = matrix.shape[1]
    width = coupling.shape[2]
    for s in range(matrix.shape[0]):
        block = matrix[s]
        high[0] = block.astype(bf16)
        bound = jnp.max(jnp.sum(jnp.abs(block), axis=0, keepdims=True))
        coarse_inverse(1, bound, lambda i: matrix[s], high, inv)
        residual_row = residual[s : s + 1, :]
        right = jnp.concatenate([coupling[s], column_of(residual_row, n)], axis=1)
        found, rest = refine(matrix[s], inv[0], right)
        solved[s] = found

        @pl.when(jnp.sum(misfits(rest, right)) > 0.0)
        def _():
            work[:, :n] = matrix[s]
            work[:, n:] = jnp.concatenate([coupling[s], column_of(residual_row, n)], axis=1)
            eliminate(work)
            solved[s] = work[:, n:]

        left = jnp.concatenate(
            [coupling[s].T, jnp.broadcast_to(residual_row, (16, n))], axis=0
        )
        product = mul3(left, solved[s][:, :width])
        top, tail = pack_symmetric(product[:width], product[width : width + 1])
        row8, _ = grid_of(8, width)
        tail = jnp.where(row8 == 2, parent[s].astype(f32), tail)
        message[s, : width // 2, :] = top
        message[s, width // 2 :, :] = tail


def node_kernel(
    sources, groups, band, slots, messages, data, answers, message, links, rights, full, high, inv, work
):
    positions = data.shape[0]
    n = data.shape[2]
    half = n // 2
    here = lax.axis_index("leaf") if positions > 1 else 0
    rows = groups * band
    for j in range(positions):
        place = pl.multiple_of((here ^ sources[j]) * band, band) if positions > 1 else 0
        for q in range(groups):
            full[q, pl.ds(place, band), :] = data[j, q * band : (q + 1) * band, :]
            links[q, pl.ds(place, band), :] = data[j, rows + q * band : rows + (q + 1) * band, :]
    shift = data[0, 2 * rows :, :]
    for j in range(1, positions):
        shift = shift + data[j, 2 * rows :, :]
    tops = [None] * groups
    tails = [None] * groups
    for j in range(messages.shape[0]):
        owner = messages[j, half + 2 : half + 3, :]
        for q in range(groups):
            hit = owner == q
            top = jnp.where(hit, messages[j, :half, :], 0.0)
            tail = jnp.where(hit, messages[j, half:, :], 0.0)
            tops[q] = top if j == 0 else tops[q] + top
            tails[q] = tail if j == 0 else tails[q] + tail
    bound = None
    vectors = []
    for q in range(groups):
        schur = full[q] + unpack_symmetric(tops[q], tails[q][1:2])
        full[q] = schur
        high[q] = schur.astype(bf16)
        size = jnp.sum(jnp.abs(schur), axis=0, keepdims=True)
        bound = size if q == 0 else jnp.maximum(bound, size)
        vector = tails[q][:1] - shift[q : q + 1]
        vectors.append(vector)
        rights[q] = jnp.concatenate([links[q], column_of(vector, n)], axis=1)
    coarse_inverse(groups, jnp.max(bound), lambda i: full[i], high, inv)
    bad = None
    for q in range(groups):
        found, rest = refine(full[q], inv[q], rights[q])
        answers[q] = found
        wrong = misfits(rest, rights[q])
        bad = wrong if q == 0 else bad + wrong

    @pl.when(jnp.sum(bad) > 0.0)
    def _():
        def one(q, carry):
            work[:, :n] = full[q]
            work[:, n:] = rights[q]
            eliminate(work)
            answers[q] = work[:, n:]
            return carry

        lax.fori_loop(0, groups, one, 0)

    width = links.shape[2]
    total = None
    for q in range(groups):
        left = jnp.concatenate([links[q].T, jnp.broadcast_to(vectors[q], (16, n))], axis=0)
        part = mul3(left, answers[q][:, :width])
        total = part if q == 0 else total + part
    top, tail = pack_symmetric(total[:width], total[width : width + 1])
    message[: width // 2, :] = top
    message[width // 2 :, :] = tail


def root_kernel(
    groups, band, parent, part, matrix, rhs, answers, solved, leaf_dir, node_dir, root_dir, full, high, inv, work
):
    size = matrix.shape[0]
    half = size // 2
    system = matrix[...] + unpack_symmetric(part[:half, :], part[half + 1 : half + 2, :])
    full[...] = system
    high[0] = system.astype(bf16)
    bound = jnp.max(jnp.sum(jnp.abs(system), axis=0, keepdims=True))
    coarse_inverse(1, bound, lambda i: full[...], high, inv)
    right = column_of(rhs[...] - part[half : half + 1, :], size)
    found, rest = refine(full[...], inv[0], right)
    work[:, size:] = found

    @pl.when(jnp.sum(misfits(rest, right)) > 0.0)
    def _():
        work[:, :size] = full[...]
        work[:, size:] = column_of(rhs[...] - part[half : half + 1, :], size)
        eliminate(work)

    answer = work[:, size:].T[:8]
    root_dir[...] = answer[:1]
    n = answers.shape[1]
    _, col = grid_of(8, 128)
    pick = (col == 0).astype(f32)
    left = jnp.concatenate([answer, pick], axis=1)
    flat = nt3(left, answers[...].reshape(groups * n, size + 128))
    every = jnp.concatenate([flat[:1, q * n : (q + 1) * n] for q in range(groups)], axis=0)
    if band == n:
        node_dir[...] = every
    else:
        me = lax.axis_index("leaf")
        moved = pltpu.roll(every, lax.rem(n - me * band, n), 1)
        node_dir[...] = moved[:, :band]
    row, _ = grid_of(groups, n)
    for s in range(solved.shape[0]):
        q = parent[s]
        own = jnp.sum(jnp.where(row == q, every, 0.0), axis=0, keepdims=True)
        left = jnp.concatenate([-jnp.broadcast_to(own, (8, n)), pick], axis=1)
        moved = nt3(left, solved[s])[:1]
        leaf_dir[s : s + 1, :] = jnp.where(q >= 0, moved, 0.0)


def gather_steps(extent):
    steps = []
    while extent > 1:
        extent //= 2
        steps.append(extent)
    return steps


def doubled(values, axis, extent):
    for distance in gather_steps(extent):
        moved = lax.ppermute(values, axis, [(i, i ^ distance) for i in range(extent)])
        values = jnp.concatenate([values, moved], axis=0)
    return values


def source_offsets(extent):
    offsets = [0]
    for distance in gather_steps(extent):
        offsets = offsets + [o ^ distance for o in offsets]
    return tuple(offsets)


def sum_over(values, axis, extent):
    if extent & (extent - 1):
        return lax.psum(values, axis)
    for distance in reversed(gather_steps(extent)):
        values = values + lax.ppermute(values, axis, [(i, i ^ distance) for i in range(extent)])
    return values


def body(
    leaves,
    sets,
    slot_parent,
    leaf_matrix,
    coupling,
    leaf_residual_rows,
    node_matrix,
    node_link,
    node_rhs,
    root_matrix,
    root_rhs,
):
    slots, n = leaf_residual_rows.shape
    groups, band, width = node_matrix.shape
    size = node_link.shape[2]
    doubling = leaves & (leaves - 1) == 0
    shape = jax.ShapeDtypeStruct
    vmem = pl.BlockSpec(memory_space=pltpu.VMEM)
    smem = pl.BlockSpec(memory_space=pltpu.SMEM)

    rank = lax.axis_index("leaf")
    placed = lax.dynamic_update_slice(
        jnp.zeros((groups, width), f32), node_rhs, (jnp.zeros((), jnp.int32), rank * band)
    )
    if doubling and band % 8 == 0:
        own = jnp.concatenate(
            [node_matrix.reshape(-1, width), node_link.reshape(-1, width), placed], axis=0
        )
        data = doubled(own[None], "leaf", leaves)
        held = band
        sources = source_offsets(leaves)
    else:
        every = lax.all_gather(
            jnp.concatenate([node_matrix, node_link], axis=0), "leaf", axis=1, tiled=True
        )
        data = jnp.concatenate(
            [every.reshape(-1, width), lax.psum(placed, "leaf")], axis=0
        )[None]
        held = width
        sources = (0,)

    solved, message = pl.pallas_call(
        leaf_kernel,
        out_shape=(
            shape((slots, n, width + 128), f32),
            shape((slots, width // 2 + 8, width), f32),
        ),
        in_specs=[smem, vmem, vmem, vmem],
        out_specs=(vmem, vmem),
        scratch_shapes=[
            pltpu.VMEM((1, n, n), bf16),
            pltpu.VMEM((1, n, n), bf16),
            pltpu.VMEM((n, n + width + 128), f32),
        ],
        name="leaf_solve",
    )(slot_parent, leaf_matrix, coupling, leaf_residual_rows)

    if doubling:
        messages = doubled(message, "leaf", leaves)
    else:
        messages = lax.all_gather(message, "leaf", axis=0, tiled=True)

    answers, part = pl.pallas_call(
        functools.partial(node_kernel, sources, groups, held, slots),
        out_shape=(
            shape((groups, width, size + 128), f32),
            shape((size // 2 + 8, size), f32),
        ),
        in_specs=[vmem, vmem],
        out_specs=(vmem, vmem),
        scratch_shapes=[
            pltpu.VMEM((groups, width, size), f32),
            pltpu.VMEM((groups, width, size + 128), f32),
            pltpu.VMEM((groups, width, width), f32),
            pltpu.VMEM((groups, width, width), bf16),
            pltpu.VMEM((groups, width, width), bf16),
            pltpu.VMEM((width, width + size + 128), f32),
        ],
        name="node_solve",
    )(messages, data)

    part = sum_over(part, "grp", sets)

    leaf_dir, node_dir, root_dir = pl.pallas_call(
        functools.partial(root_kernel, groups, band),
        out_shape=(
            shape((slots, n), f32),
            shape((groups, band), f32),
            shape((1, size), f32),
        ),
        in_specs=[smem, vmem, vmem, vmem, vmem, vmem],
        out_specs=(vmem, vmem, vmem),
        scratch_shapes=[
            pltpu.VMEM((size, size), f32),
            pltpu.VMEM((1, size, size), bf16),
            pltpu.VMEM((1, size, size), bf16),
            pltpu.VMEM((size, size + 128), f32),
        ],
        name="root_solve",
    )(slot_parent, part, root_matrix, root_rhs[None, :], answers, solved)
    return leaf_dir, node_dir, root_dir[0]


def solution(mesh):
    return jax.shard_map(
        functools.partial(body, mesh.shape["leaf"], mesh.shape["grp"]),
        mesh=mesh,
        in_specs=(
            P(("leaf", "grp")),
            P(("leaf", "grp"), None, None),
            P(("leaf", "grp"), None, None),
            P(("leaf", "grp"), None),
            P("grp", "leaf", None),
            P("grp", "leaf", None),
            P("grp", "leaf"),
            P(),
            P(),
        ),
        out_specs=(P(("leaf", "grp"), None), P("grp", "leaf"), P()),
        check_vma=False,
    )
```

```python
import functools

import jax
import jax.numpy as jnp
from jax import lax
from jax.experimental import pallas as pl
from jax.experimental.pallas import tpu as pltpu
from jax.sharding import PartitionSpec as P

f32 = jnp.float32
bf16 = jnp.bfloat16
FLOOR = 0.1
COARSE = 0.04
MOST_STEPS = 24
KERNEL_VMEM = 24 << 20
ACCEPT = 4e-8


def mul(a, b):
    return jnp.dot(a, b, preferred_element_type=f32)


def split(a):
    high = a.astype(bf16)
    return high, (a - high.astype(f32)).astype(bf16)


def split3(a):
    high = a.astype(bf16)
    rest = a - high.astype(f32)
    mid = rest.astype(bf16)
    return high, mid, (rest - mid.astype(f32)).astype(bf16)


def beside(*parts):
    return jnp.concatenate(parts, axis=1)


def above(*parts):
    return jnp.concatenate(parts, axis=0)


def mul3(a, b):
    ah, al = split(a)
    bh, bl = split(b)
    return mul(beside(ah, ah, al), above(bh, bl, bh))


def grid_of(rows, cols):
    return (
        lax.broadcasted_iota(jnp.int32, (rows, cols), 0),
        lax.broadcasted_iota(jnp.int32, (rows, cols), 1),
    )


def identity(n):
    row, col = grid_of(n, n)
    return (row == col).astype(f32)


def pack_symmetric(full, extra):
    n = full.shape[0]
    half = n // 2
    row, col = grid_of(half, n)
    lower = full[half:]
    moved = pltpu.roll(lower, half, 1)
    top = jnp.where(col < row, moved, full[:half])
    diagonal = jnp.sum(jnp.where(col == row + half, lower, 0.0), axis=0, keepdims=True)
    row8, _ = grid_of(8, n)
    tail = jnp.where(row8 == 0, jnp.broadcast_to(extra, (8, n)), 0.0)
    tail = jnp.where(row8 == 1, jnp.broadcast_to(diagonal, (8, n)), tail)
    return top, tail


def unpack_symmetric(top, diagonal):
    half, n = top.shape
    row, col = grid_of(half, n)
    flipped = jnp.concatenate([top, jnp.zeros_like(top)], axis=0).T
    upper = jnp.where((col < half) & (col < row), flipped[:half], top)
    inner = pltpu.roll(jnp.where(col < row, top, flipped[:half]), half, 1)
    inner = jnp.where(col == row + half, jnp.broadcast_to(diagonal, (half, n)), inner)
    lower = jnp.where(col < half, flipped[half:], inner)
    return jnp.concatenate([upper, lower], axis=0)


def coarse_inverse(count, bound, matrix_of, high, inv):
    n = high.shape[1]
    delta = (bound - FLOOR) / (bound + FLOOR)
    alpha = 2.0 / (bound + FLOOR)
    scale = alpha * 2.0 / (2.0 - delta * delta)
    for i in range(count):
        inv[i] = (scale * (2.0 * identity(n) - alpha * matrix_of(i))).astype(bf16)

    def step(carry):
        delta, count_left = carry
        scale = 2.0 / (2.0 - delta * delta)
        now = [inv[i] for i in range(count)]
        error = [(identity(n) - mul(now[i], high[i])).astype(bf16) for i in range(count)]
        for i in range(count):
            inv[i] = (scale * (now[i].astype(f32) + mul(error[i], now[i]))).astype(bf16)
        return delta * delta / (2.0 - delta * delta), count_left - 1

    start = (delta * delta / (2.0 - delta * delta), jnp.int32(MOST_STEPS))
    lax.while_loop(lambda c: (c[0] > COARSE) & (c[1] > 0), step, start)


def refine(matrices, inverses, rights):
    pieces = [split3(m) for m in matrices]
    step0 = [mul(r.astype(bf16), v).astype(bf16) for r, v in zip(rights, inverses)]
    rest = [
        r - mul(beside(s, s, s), above(*p)) for r, s, p in zip(rights, step0, pieces)
    ]
    step1 = [mul(r.astype(bf16), v).astype(bf16) for r, v in zip(rest, inverses)]
    rest = [r - mul(beside(s, s), above(*p[:2])) for r, s, p in zip(rest, step1, pieces)]
    step2 = [mul(r.astype(bf16), v).astype(bf16) for r, v in zip(rest, inverses)]
    rest = [r - mul(beside(s, s), above(*p[:2])) for r, s, p in zip(rest, step2, pieces)]
    step3 = [mul(r.astype(bf16), v) for r, v in zip(rest, inverses)]
    found = [
        a.astype(f32) + (b.astype(f32) + (c.astype(f32) + d))
        for a, b, c, d in zip(step0, step1, step2, step3)
    ]
    return found, rest


def misfits(rest, right):
    got = jnp.sum(rest * rest, axis=1, keepdims=True)
    allowed = ACCEPT * jnp.sum(right * right, axis=1, keepdims=True)
    return jnp.where(got <= allowed, 0.0, 1.0)


def eliminate(work):
    n, width = work.shape

    def step(k, carry):
        row, col = grid_of(8, width)
        base = pl.multiple_of((k // 8) * 8, 8)
        block = work[pl.ds(base, 8), :]
        pivot_row = jnp.sum(jnp.where(row == k - base, block, 0.0), axis=0, keepdims=True)
        pivot = jnp.sum(jnp.where(col[:1] == k, pivot_row, 0.0), axis=1, keepdims=True)
        scaled = pivot_row / pivot
        full = work[...]
        row, col = grid_of(n, width)
        column = jnp.sum(jnp.where(col == k, full, 0.0), axis=1, keepdims=True)
        work[...] = jnp.where(row == k, scaled, full - column * scaled)
        return carry

    lax.fori_loop(0, n, step, 0)


def solve_again(work, matrix, right):
    n, rows = matrix.shape[0], right.shape[0]
    work[:, :n] = matrix
    padded = above(right, jnp.zeros((work.shape[1] - n - rows, n), f32))
    work[:, n:] = padded.T
    eliminate(work)
    return work[:, n:].T[:rows]


def norm_bound(matrix):
    return jnp.sum(jnp.abs(matrix), axis=0, keepdims=True)


def leaf_kernel(parent, matrix, coupling, residual, solved, message, high, inv, work):
    n = matrix.shape[1]
    width = coupling.shape[2]
    for s in range(matrix.shape[0]):
        block = matrix[s]
        high[0] = block.astype(bf16)
        coarse_inverse(1, jnp.max(norm_bound(block)), lambda i: matrix[s], high, inv)
        right = above(coupling[s].T, jnp.broadcast_to(residual[s : s + 1, :], (16, n)))
        found, rest = refine([matrix[s]], [inv[0]], [right])
        solved[s] = found[0]

        @pl.when(jnp.sum(misfits(rest[0], right)) > 0.0)
        def _():
            right = above(coupling[s].T, jnp.broadcast_to(residual[s : s + 1, :], (16, n)))
            solved[s] = solve_again(work, matrix[s], right)

        product = mul3(solved[s], coupling[s])
        top, tail = pack_symmetric(product[:width], product[width : width + 1])
        row8, _ = grid_of(8, width)
        tail = jnp.where(row8 == 2, parent[s].astype(f32), tail)
        message[s, : width // 2, :] = top
        message[s, width // 2 :, :] = tail


def node_kernel(sources, groups, band, counts, *refs):
    messages, data = refs[: counts[0]], refs[counts[0] : sum(counts)]
    answers, message, links, full, high, inv, work = refs[sum(counts) :]
    n = full.shape[1]
    width = links.shape[2]
    half = n // 2
    rows = groups * band
    here = lax.axis_index("leaf") if len(sources) > 1 else 0
    at = 0
    shift = None
    for piece in data:
        for j in range(piece.shape[0]):
            place = pl.multiple_of((here ^ sources[at]) * band, band) if len(sources) > 1 else 0
            at += 1
            for q in range(groups):
                full[q, pl.ds(place, band), :] = piece[j, q * band : (q + 1) * band, :]
                links[q, pl.ds(place, band), :] = piece[j, rows + q * band : rows + (q + 1) * band, :]
            last = piece[j, 2 * rows :, :]
            shift = last if shift is None else shift + last
    tops = [jnp.zeros((half, n), f32)] * groups
    tails = [jnp.zeros((8, n), f32)] * groups
    for piece in messages:
        for j in range(piece.shape[0]):
            owner = piece[j, half + 2 : half + 3, :]
            for q in range(groups):
                hit = owner == q
                tops[q] = tops[q] + jnp.where(hit, piece[j, :half, :], 0.0)
                tails[q] = tails[q] + jnp.where(hit, piece[j, half:, :], 0.0)
    bound = None
    vectors = []
    for q in range(groups):
        schur = full[q] + unpack_symmetric(tops[q], tails[q][1:2])
        full[q] = schur
        high[q] = schur.astype(bf16)
        size = norm_bound(schur)
        bound = size if q == 0 else jnp.maximum(bound, size)
        vectors.append(jnp.broadcast_to(tails[q][:1] - shift[q : q + 1], (16, n)))
    coarse_inverse(groups, jnp.max(bound), lambda i: full[i], high, inv)
    rights = [above(links[q].T, vectors[q]) for q in range(groups)]
    found, rest = refine(
        [full[q] for q in range(groups)], [inv[q] for q in range(groups)], rights
    )
    bad = None
    for q in range(groups):
        answers[q] = found[q]
        wrong = misfits(rest[q], rights[q])
        bad = wrong if q == 0 else bad + wrong

    @pl.when(jnp.sum(bad) > 0.0)
    def _():
        for q in range(groups):
            answers[q] = solve_again(work, full[q], above(links[q].T, vectors[q]))

    total = None
    for q in range(groups):
        part = mul3(answers[q], links[q])
        total = part if q == 0 else total + part
    top, tail = pack_symmetric(total[:width], total[width : width + 1])
    message[: width // 2, :] = top
    message[width // 2 :, :] = tail


def root_kernel(
    groups, band, count, parent, matrix, rhs, answers, solved, *refs
):
    parts = refs[:count]
    leaf_dir, node_dir, root_dir, full, high, inv, work, found_root = refs[count:]
    size = matrix.shape[0]
    half = size // 2
    n = answers.shape[2]
    part = parts[0][...]
    for other in parts[1:]:
        part = part + other[...]
    system = matrix[...] + unpack_symmetric(part[:half, :], part[half + 1 : half + 2, :])
    full[...] = system
    high[0] = system.astype(bf16)
    coarse_inverse(1, jnp.max(norm_bound(system)), lambda i: full[...], high, inv)
    right = jnp.broadcast_to(rhs[...] - part[half : half + 1, :], (16, size))
    found, rest = refine([full[...]], [inv[0]], [right])
    found_root[...] = found[0]

    @pl.when(jnp.sum(misfits(rest[0], right)) > 0.0)
    def _():
        found_root[...] = solve_again(work, full[...], right)

    answer = found_root[...]
    root_dir[...] = answer[:1]
    moves = [mul3(answer, answers[q][:size])[:1] + answers[q][size : size + 1] for q in range(groups)]
    every = above(*moves)
    if band == n:
        node_dir[...] = every
    else:
        me = lax.axis_index("leaf")
        node_dir[...] = pltpu.roll(every, lax.rem(n - me * band, n), 1)[:, :band]
    row, _ = grid_of(groups, n)
    for s in range(solved.shape[0]):
        q = parent[s]
        own = jnp.sum(jnp.where(row == q, every, 0.0), axis=0, keepdims=True)
        moved = mul3(jnp.broadcast_to(own, (16, n)), solved[s][:n])
        moved = solved[s][n : n + 1] - moved[:1]
        leaf_dir[s : s + 1, :] = jnp.where(q >= 0, moved, 0.0)


def gather_steps(extent):
    steps = []
    while extent > 1:
        extent //= 2
        steps.append(extent)
    return steps


def doubled(values, axis, extent):
    pieces = [values]
    for distance in gather_steps(extent):
        sent = pieces[0] if len(pieces) == 1 else jnp.concatenate(pieces, axis=0)
        pieces.append(lax.ppermute(sent, axis, [(i, i ^ distance) for i in range(extent)]))
    return pieces


def source_offsets(extent):
    offsets = [0]
    for distance in gather_steps(extent):
        offsets = offsets + [o ^ distance for o in offsets]
    return tuple(offsets)


def sum_parts(values, axis, extent):
    if extent & (extent - 1):
        return [lax.psum(values, axis)]
    steps = gather_steps(extent)
    for i, distance in enumerate(reversed(steps)):
        moved = lax.ppermute(values, axis, [(i, i ^ distance) for i in range(extent)])
        if i + 1 == len(steps):
            return [values, moved]
        values = values + moved
    return [values]


def local(*values):
    return [pltpu.with_memory_space_constraint(v, pltpu.VMEM) for v in values]


def body(
    leaves,
    sets,
    slot_parent,
    leaf_matrix,
    coupling,
    leaf_residual_rows,
    node_matrix,
    node_link,
    node_rhs,
    root_matrix,
    root_rhs,
):
    slots, n = leaf_residual_rows.shape
    groups, band, width = node_matrix.shape
    size = node_link.shape[2]
    doubling = leaves & (leaves - 1) == 0
    vmem = pl.BlockSpec(memory_space=pltpu.VMEM)
    smem = pl.BlockSpec(memory_space=pltpu.SMEM)
    params = pltpu.CompilerParams(vmem_limit_bytes=KERNEL_VMEM)

    rank = lax.axis_index("leaf")
    placed = lax.dynamic_update_slice(
        jnp.zeros((groups, width), f32), node_rhs, (jnp.zeros((), jnp.int32), rank * band)
    )
    if doubling and band % 8 == 0:
        own = jnp.concatenate(
            [node_matrix.reshape(-1, width), node_link.reshape(-1, width), placed], axis=0
        )
        data = doubled(own[None], "leaf", leaves)
        held = band
        sources = source_offsets(leaves)
    else:
        every = lax.all_gather(
            jnp.concatenate([node_matrix, node_link], axis=0), "leaf", axis=1, tiled=True
        )
        data = [
            jnp.concatenate([every.reshape(-1, width), lax.psum(placed, "leaf")], axis=0)[None]
        ]
        held = width
        sources = (0,)

    solved, message = pl.pallas_call(
        leaf_kernel,
        out_shape=(
            pltpu.VMEM((slots, width + 16, n), f32),
            pltpu.VMEM((slots, width // 2 + 8, width), f32),
        ),
        in_specs=[smem, vmem, vmem, vmem],
        out_specs=(vmem, vmem),
        scratch_shapes=[
            pltpu.VMEM((1, n, n), bf16),
            pltpu.VMEM((1, n, n), bf16),
            pltpu.VMEM((n, n + 2 * width), f32),
        ],
        compiler_params=params,
        name="leaf_solve",
    )(slot_parent, leaf_matrix, coupling, leaf_residual_rows)

    if doubling:
        messages = doubled(message, "leaf", leaves)
    else:
        messages = [lax.all_gather(message, "leaf", axis=0, tiled=True)]

    answers, part = pl.pallas_call(
        functools.partial(node_kernel, sources, groups, held, (len(messages), len(data))),
        out_shape=(
            pltpu.VMEM((groups, size + 16, width), f32),
            pltpu.VMEM((size // 2 + 8, size), f32),
        ),
        in_specs=[vmem] * (len(messages) + len(data)),
        out_specs=(vmem, vmem),
        scratch_shapes=[
            pltpu.VMEM((groups, width, size), f32),
            pltpu.VMEM((groups, width, width), f32),
            pltpu.VMEM((groups, width, width), bf16),
            pltpu.VMEM((groups, width, width), bf16),
            pltpu.VMEM((width, width + 2 * size), f32),
        ],
        compiler_params=params,
        name="node_solve",
    )(*local(*messages, *data))

    parts = sum_parts(part, "grp", sets)

    leaf_dir, node_dir, root_dir = pl.pallas_call(
        functools.partial(root_kernel, groups, band, len(parts)),
        out_shape=(
            jax.ShapeDtypeStruct((slots, n), f32),
            jax.ShapeDtypeStruct((groups, band), f32),
            jax.ShapeDtypeStruct((1, size), f32),
        ),
        in_specs=[smem] + [vmem] * (4 + len(parts)),
        out_specs=(vmem, vmem, vmem),
        scratch_shapes=[
            pltpu.VMEM((size, size), f32),
            pltpu.VMEM((1, size, size), bf16),
            pltpu.VMEM((1, size, size), bf16),
            pltpu.VMEM((size, 2 * size), f32),
            pltpu.VMEM((16, size), f32),
        ],
        compiler_params=params,
        name="root_solve",
    )(slot_parent, root_matrix, root_rhs[None, :], *local(answers, solved, *parts))
    return leaf_dir, node_dir, root_dir[0]


def solution(mesh):
    return jax.shard_map(
        functools.partial(body, mesh.shape["leaf"], mesh.shape["grp"]),
        mesh=mesh,
        in_specs=(
            P(("leaf", "grp")),
            P(("leaf", "grp"), None, None),
            P(("leaf", "grp"), None, None),
            P(("leaf", "grp"), None),
            P("grp", "leaf", None),
            P("grp", "leaf", None),
            P("grp", "leaf"),
            P(),
            P(),
        ),
        out_specs=(P(("leaf", "grp"), None), P("grp", "leaf"), P()),
        check_vma=False,
    )
```

```python
import functools

import jax
import jax.numpy as jnp
from jax import lax
from jax.experimental import pallas as pl
from jax.experimental.pallas import tpu as pltpu
from jax.sharding import PartitionSpec as P

f32 = jnp.float32
bf16 = jnp.bfloat16
FLOOR = 0.1
STEPS = 5
ROOT_STEPS = 6
COST = 3_000_000_000
KERNEL_VMEM = 24 << 20
ACCEPT = 4e-5


def mul(a, b):
    return jnp.dot(a, b, preferred_element_type=f32)


def split(a):
    high = a.astype(bf16)
    return high, (a - high.astype(f32)).astype(bf16)


def split3(a):
    high = a.astype(bf16)
    rest = a - high.astype(f32)
    mid = rest.astype(bf16)
    return high, mid, (rest - mid.astype(f32)).astype(bf16)


def beside(*parts):
    return jnp.concatenate(parts, axis=1)


def above(*parts):
    return jnp.concatenate(parts, axis=0)


def mul3(a, b):
    ah, al = split(a)
    bh, bl = split(b)
    return mul(beside(ah, ah, al), above(bh, bl, bh))


def grid_of(rows, cols):
    return (
        lax.broadcasted_iota(jnp.int32, (rows, cols), 0),
        lax.broadcasted_iota(jnp.int32, (rows, cols), 1),
    )


def identity(n):
    row, col = grid_of(n, n)
    return (row == col).astype(f32)


def pack_symmetric(full, extra):
    n = full.shape[0]
    half = n // 2
    row, col = grid_of(half, n)
    lower = full[half:]
    moved = pltpu.roll(lower, half, 1)
    top = jnp.where(col < row, moved, full[:half])
    diagonal = jnp.sum(jnp.where(col == row + half, lower, 0.0), axis=0, keepdims=True)
    row8, _ = grid_of(8, n)
    tail = jnp.where(row8 == 0, jnp.broadcast_to(extra, (8, n)), 0.0)
    tail = jnp.where(row8 == 1, jnp.broadcast_to(diagonal, (8, n)), tail)
    return top, tail


def unpack_symmetric(top, diagonal):
    half, n = top.shape
    row, col = grid_of(half, n)
    flipped = jnp.concatenate([top, jnp.zeros_like(top)], axis=0).T
    upper = jnp.where((col < half) & (col < row), flipped[:half], top)
    inner = pltpu.roll(jnp.where(col < row, top, flipped[:half]), half, 1)
    inner = jnp.where(col == row + half, jnp.broadcast_to(diagonal, (half, n)), inner)
    lower = jnp.where(col < half, flipped[half:], inner)
    return jnp.concatenate([upper, lower], axis=0)


def coarse_inverse(bound, matrices, steps):
    one = identity(matrices[0].shape[0])
    alpha = 2.0 / (bound + FLOOR)
    delta = (bound - FLOOR) / (bound + FLOOR)
    square = delta * delta
    scale = 2.0 / (2.0 - square)
    scaled = [alpha * m for m in matrices]
    errors = [(one - s).astype(bf16) for s in scaled]
    inverses = [((scale * alpha) * (2.0 * one - s)).astype(bf16) for s in scaled]
    for _ in range(steps - 1):
        errors = [(scale * (mul(e, e) - (0.5 * square) * one)).astype(bf16) for e in errors]
        delta = square / (2.0 - square)
        square = delta * delta
        scale = 2.0 / (2.0 - square)
        inverses = [
            (scale * (v.astype(f32) + mul(e, v))).astype(bf16) for e, v in zip(errors, inverses)
        ]
    return inverses


def finish(matrices, inverses, rights):
    errors = [
        identity(m.shape[0]) - mul(beside(v, v, v), above(*split3(m)))
        for m, v in zip(matrices, inverses)
    ]
    pieces = [split(e) for e in errors]
    squares = [mul(h, h).astype(bf16) for h, _ in pieces]
    first = []
    for right, (eh, el) in zip(rights, pieces):
        rh, rl = split(right)
        first.append(right + mul(beside(rh, rh, rl), above(eh, el, eh)))
    second = [mul(z.astype(bf16), s) for z, s in zip(first, squares)]
    found = [
        mul(beside(*split3(z + d)), above(v, v, v)) for z, d, v in zip(first, second, inverses)
    ]
    return found, [misfits(d, z) for z, d in zip(first, second)]


def misfits(change, values):
    got = jnp.sum(change * change, axis=1, keepdims=True)
    allowed = ACCEPT * jnp.sum(values * values, axis=1, keepdims=True)
    return jnp.where(got <= allowed, 0.0, 1.0)


def eliminate(work):
    n, width = work.shape

    def step(k, carry):
        row, col = grid_of(8, width)
        base = pl.multiple_of((k // 8) * 8, 8)
        block = work[pl.ds(base, 8), :]
        pivot_row = jnp.sum(jnp.where(row == k - base, block, 0.0), axis=0, keepdims=True)
        pivot = jnp.sum(jnp.where(col[:1] == k, pivot_row, 0.0), axis=1, keepdims=True)
        scaled = pivot_row / pivot
        full = work[...]
        row, col = grid_of(n, width)
        column = jnp.sum(jnp.where(col == k, full, 0.0), axis=1, keepdims=True)
        work[...] = jnp.where(row == k, scaled, full - column * scaled)
        return carry

    lax.fori_loop(0, n, step, 0)


def solve_again(work, matrix, right):
    n, rows = matrix.shape[0], right.shape[0]
    work[:, :n] = matrix
    padded = above(right, jnp.zeros((work.shape[1] - n - rows, n), f32))
    work[:, n:] = padded.T
    eliminate(work)
    return work[:, n:].T[:rows]


def norm_bound(*matrices):
    sums = [jnp.sum(jnp.abs(m), axis=0, keepdims=True) for m in matrices]
    most = sums[0]
    for other in sums[1:]:
        most = jnp.maximum(most, other)
    return jnp.max(most, axis=1, keepdims=True)


def stage_kernel(parent, matrix, link, rhs, owners, own, matrix_rows, link_rows, rhs_rows, sems):
    copies = [
        pltpu.make_async_copy(source, target, sems.at[i])
        for i, (source, target) in enumerate(
            ((matrix, matrix_rows), (link, link_rows), (rhs, rhs_rows))
        )
    ]
    for copy in copies:
        copy.start()
    for s in range(owners.shape[0]):
        owners[s] = jnp.full(owners.shape[1:], parent[s].astype(f32))
    groups, band, _ = matrix_rows.shape
    rows = groups * band
    own[0, 2 * rows :, :] = jnp.zeros((groups, own.shape[2]), f32)
    for copy in copies:
        copy.wait()
    for q in range(groups):
        own[0, q * band : (q + 1) * band, :] = matrix_rows[q]
        own[0, rows + q * band : rows + (q + 1) * band, :] = link_rows[q]
    own[0, 2 * rows :, :band] = rhs_rows[...]


def invert_kernel(*refs):
    count = (len(refs) - 2) // 2
    inputs, outputs, (inverse, sems) = refs[:count], refs[count:-2], refs[-2:]
    copies = [
        pltpu.make_async_copy(source, target, sems.at[i])
        for i, (source, target) in enumerate(zip(inputs, outputs))
    ]
    for copy in copies:
        copy.start()
    copies[0].wait()
    matrix = outputs[0]
    for s in range(matrix.shape[0]):
        block = matrix[s]
        inverse[s] = coarse_inverse(norm_bound(block), [block], STEPS)[0]
    for copy in copies[1:]:
        copy.wait()


def leaf_kernel(owners, matrix, coupling, residual, inverse, solved, message, work):
    n = matrix.shape[1]
    width = coupling.shape[2]
    for s in range(matrix.shape[0]):
        right = above(coupling[s].T, jnp.broadcast_to(residual[s : s + 1, :], (16, n)))
        found, bad = finish([matrix[s]], [inverse[s]], [right])
        solved[s] = found[0]

        @pl.when(jnp.sum(bad[0]) > 0.0)
        def _():
            right = above(coupling[s].T, jnp.broadcast_to(residual[s : s + 1, :], (16, n)))
            solved[s] = solve_again(work, matrix[s], right)

        product = mul3(solved[s], coupling[s])
        top, tail = pack_symmetric(product[:width], product[width : width + 1])
        row8, _ = grid_of(8, width)
        tail = jnp.where(row8 == 2, owners[s], tail)
        message[s, : width // 2, :] = top
        message[s, width // 2 :, :] = tail


def assemble_kernel(sources, groups, band, *refs):
    data = refs[:-3]
    full, links, shift = refs[-3:]
    rows = groups * band
    here = lax.axis_index("leaf") if len(sources) > 1 else 0
    at = 0
    total = None
    for piece in data:
        for j in range(piece.shape[0]):
            place = pl.multiple_of((here ^ sources[at]) * band, band) if len(sources) > 1 else 0
            at += 1
            for q in range(groups):
                full[q, pl.ds(place, band), :] = piece[j, q * band : (q + 1) * band, :]
                links[q, pl.ds(place, band), :] = piece[j, rows + q * band : rows + (q + 1) * band, :]
            last = piece[j, 2 * rows :, :]
            if len(sources) > 1:
                last = pltpu.roll(last, place, 1)
            total = last if total is None else total + last
    shift[...] = total


def node_kernel(regular, links, shift, *refs):
    messages = refs[:-5]
    answers, message, full, rights, work = refs[-5:]
    groups, n, width = links.shape
    half = n // 2
    tops = [jnp.zeros((half, n), f32)] * groups
    tails = [jnp.zeros((8, n), f32)] * groups
    for piece in messages:
        for j in range(piece.shape[0]):
            owner = piece[j, half + 2 : half + 3, :]
            for q in range(groups):
                hit = owner == q
                tops[q] = tops[q] + jnp.where(hit, piece[j, :half, :], 0.0)
                tails[q] = tails[q] + jnp.where(hit, piece[j, half:, :], 0.0)
    for q in range(groups):
        full[q] = regular[q] + unpack_symmetric(tops[q], tails[q][1:2])
        rights[q, :width] = links[q].T
        rights[q, width:] = jnp.broadcast_to(tails[q][:1] - shift[q : q + 1], (16, n))
    blocks = [full[q] for q in range(groups)]
    inverses = coarse_inverse(norm_bound(*blocks), blocks, STEPS)
    found, bad = finish(blocks, inverses, [rights[q] for q in range(groups)])
    for q in range(groups):
        answers[q] = found[q]

    @pl.when(jnp.sum(sum(bad)) > 0.0)
    def _():
        for q in range(groups):
            answers[q] = solve_again(work, full[q], rights[q])

    total = None
    for q in range(groups):
        part = mul3(answers[q], links[q])
        total = part if q == 0 else total + part
    top, tail = pack_symmetric(total[:width], total[width : width + 1])
    message[: width // 2, :] = top
    message[width // 2 :, :] = tail


def prepare_kernel(
    owners, part, matrix, rhs, answers, solved, base, base_row, moves, fixed, leaf_moves, leaf_fixed
):
    size = matrix.shape[0]
    half = size // 2
    groups, _, n = answers.shape
    base[...] = matrix[...] + unpack_symmetric(part[:half, :], part[half + 1 : half + 2, :])
    base_row[...] = jnp.broadcast_to(rhs[...] - part[half : half + 1, :], base_row.shape)
    for q in range(groups):
        fixed[q : q + 1, :] = answers[q, size : size + 1, :]
        moves[q] = answers[q, :size, :]
    for s in range(solved.shape[0]):
        owner = owners[s, :1, :1]
        own = jnp.zeros_like(answers[0])
        for q in range(groups):
            own = jnp.where(owner == q, answers[q], own)
        product = mul3(own, solved[s, :n, :])
        live = owner >= 0.0
        leaf_moves[s] = jnp.where(live, -product[:size], 0.0)
        last = solved[s, n : n + 8, :] - product[size : size + 8]
        leaf_fixed[s] = jnp.where(live, last, 0.0)


def root_kernel(
    band, base, base_row, moves, fixed, leaf_moves, leaf_fixed, *refs
):
    others = refs[:-6]
    leaf_dir, node_dir, root_dir, full, found_root, work = refs[-6:]
    size = base.shape[0]
    half = size // 2
    groups, _, n = moves.shape
    system = base[...]
    right = base_row[...]
    for other in others:
        system = system + unpack_symmetric(other[:half, :], other[half + 1 : half + 2, :])
        right = right - other[half : half + 1, :]
    full[...] = system
    inverses = coarse_inverse(norm_bound(system), [system], ROOT_STEPS)
    found, bad = finish([system], inverses, [right])
    found_root[...] = found[0]

    @pl.when(jnp.sum(bad[0]) > 0.0)
    def _():
        found_root[...] = solve_again(work, full[...], right)

    answer = found_root[:1, :]
    root_dir[...] = answer
    column = jnp.broadcast_to(answer, (size, size)).T
    each = [jnp.sum(column * moves[q], axis=0, keepdims=True) for q in range(groups)]
    every = above(*each) + fixed[...]
    if band == n:
        node_dir[...] = every
    else:
        me = lax.axis_index("leaf")
        node_dir[...] = pltpu.roll(every, lax.rem(n - me * band, n), 1)[:, :band]
    wide = leaf_moves.shape[2] // size
    for s in range(leaf_moves.shape[0]):
        terms = beside(*[column] * wide) * leaf_moves[s]
        leaf_dir[s : s + 1, :] = jnp.sum(terms, axis=0, keepdims=True) + leaf_fixed[s, :1, :]


def gather_steps(extent):
    steps = []
    while extent > 1:
        extent //= 2
        steps.append(extent)
    return steps


def moved(values, axis, extent, distance):
    return lax.ppermute(values, axis, [(i, i ^ distance) for i in range(extent)])


def exchange(pieces, axis, extent, distance):
    sent = pieces[0] if len(pieces) == 1 else jnp.concatenate(pieces, axis=0)
    pieces.append(moved(sent, axis, extent, distance))


def doubled(values, axis, extent):
    pieces = [values]
    for distance in gather_steps(extent):
        exchange(pieces, axis, extent, distance)
    return pieces


def after(value, pieces):
    value, pieces[-1] = lax.optimization_barrier((value, pieces[-1]))
    return value


def source_offsets(steps):
    offsets = [0]
    for distance in steps:
        offsets = offsets + [o ^ distance for o in offsets]
    return tuple(offsets)


def other_parts(values, axis, extent):
    if extent == 1:
        return []
    if extent & (extent - 1):
        return [lax.psum(values, axis) - values]
    steps = gather_steps(extent)
    pieces = []
    for distance in reversed(steps):
        pieces.append(moved(values, axis, extent, distance))
        values = values + pieces[-1]
    return pieces


def remote(*values):
    return [pltpu.with_memory_space_constraint(v, pltpu.HBM) for v in values]


def local(*values):
    return [pltpu.with_memory_space_constraint(v, pltpu.VMEM) for v in values]


def body(
    leaves,
    sets,
    slot_parent,
    leaf_matrix,
    coupling,
    leaf_residual_rows,
    node_matrix,
    node_link,
    node_rhs,
    root_matrix,
    root_rhs,
):
    slots, n = leaf_residual_rows.shape
    groups, band, width = node_matrix.shape
    size = node_link.shape[2]
    doubling = leaves & (leaves - 1) == 0
    vmem = pl.BlockSpec(memory_space=pltpu.VMEM)
    smem = pl.BlockSpec(memory_space=pltpu.SMEM)
    params = pltpu.CompilerParams(vmem_limit_bytes=KERNEL_VMEM)

    paced = doubling and band % 8 == 0
    hbm = pl.BlockSpec(memory_space=pltpu.HBM)
    nodes = [node_matrix, node_link, node_rhs]
    owners, own = pl.pallas_call(
        stage_kernel,
        out_shape=(
            pltpu.VMEM((slots, 8, width), f32),
            pltpu.VMEM((1, 2 * groups * band + groups, width), f32),
        ),
        in_specs=[smem, hbm, hbm, hbm],
        out_specs=(vmem, vmem),
        scratch_shapes=[pltpu.VMEM(a.shape, f32) for a in nodes] + [pltpu.SemaphoreType.DMA((3,))],
        compiler_params=params,
        name="stage",
    )(slot_parent, *remote(*nodes))
    if paced:
        data = [own]
        order = [4, 8, 2, 1]
        held = band
        sources = source_offsets(order)
    else:
        rank = lax.axis_index("leaf")
        placed = lax.dynamic_update_slice(
            jnp.zeros((groups, width), f32), node_rhs, (jnp.zeros((), jnp.int32), rank * band)
        )
        every = lax.all_gather(
            jnp.concatenate([node_matrix, node_link], axis=0), "leaf", axis=1, tiled=True
        )
        data = [
            jnp.concatenate([every.reshape(-1, width), lax.psum(placed, "leaf")], axis=0)[None]
        ]
        held = width
        sources = (0,)

    if paced:
        exchange(data, "leaf", leaves, 4)
    staged = [leaf_matrix, coupling, leaf_residual_rows, root_matrix, root_rhs[None, :]]
    leaf_matrix, coupling, leaf_residual_rows, root_matrix, root_row, inverse = pl.pallas_call(
        invert_kernel,
        out_shape=[pltpu.VMEM(a.shape, f32) for a in staged] + [pltpu.VMEM((slots, n, n), bf16)],
        in_specs=[hbm] * len(staged),
        out_specs=[vmem] * (len(staged) + 1),
        scratch_shapes=[pltpu.SemaphoreType.DMA((len(staged),))],
        compiler_params=params,
        cost_estimate=pl.CostEstimate(flops=COST, bytes_accessed=0, transcendentals=0),
        name="leaf_invert",
    )(*remote(*staged))
    if paced:
        inverse = after(inverse, data)
        exchange(data, "leaf", leaves, 8)
    solved, message = pl.pallas_call(
        leaf_kernel,
        out_shape=(
            pltpu.VMEM((slots, width + 16, n), f32),
            pltpu.VMEM((slots, width // 2 + 8, width), f32),
        ),
        in_specs=[vmem] * 5,
        out_specs=(vmem, vmem),
        scratch_shapes=[
            pltpu.VMEM((n, n + 2 * width), f32),
        ],
        compiler_params=params,
        cost_estimate=pl.CostEstimate(flops=COST, bytes_accessed=0, transcendentals=0),
        name="leaf_solve",
    )(*local(owners, leaf_matrix, coupling, leaf_residual_rows, inverse))
    if paced:
        messages = [message]
        exchange(messages, "leaf", leaves, 2)
        messages[-1] = after(messages[-1], data)
        exchange(data, "leaf", leaves, 2)
        exchange(messages, "leaf", leaves, 8)
        exchange(messages, "leaf", leaves, 4)
        messages[-1] = after(messages[-1], data)
        exchange(messages, "leaf", leaves, 1)
        exchange(data, "leaf", leaves, 1)
    elif doubling:
        messages = doubled(message, "leaf", leaves)
    else:
        messages = [lax.all_gather(message, "leaf", axis=0, tiled=True)]

    node_blocks = pl.pallas_call(
        functools.partial(assemble_kernel, sources, groups, held),
        out_shape=(
            pltpu.VMEM((groups, width, width), f32),
            pltpu.VMEM((groups, width, size), f32),
            pltpu.VMEM((groups, width), f32),
        ),
        in_specs=[vmem] * len(data),
        out_specs=(vmem, vmem, vmem),
        compiler_params=params,
        name="node_assemble",
    )(*local(*data))

    answers, part = pl.pallas_call(
        node_kernel,
        out_shape=(
            pltpu.VMEM((groups, size + 16, width), f32),
            pltpu.VMEM((size // 2 + 8, size), f32),
        ),
        in_specs=[vmem] * (3 + len(messages)),
        out_specs=(vmem, vmem),
        scratch_shapes=[
            pltpu.VMEM((groups, width, width), f32),
            pltpu.VMEM((groups, size + 16, width), f32),
            pltpu.VMEM((width, width + 2 * size), f32),
        ],
        compiler_params=params,
        name="node_solve",
    )(*local(*node_blocks, *messages))

    others = other_parts(part, "grp", sets)
    prepared = pl.pallas_call(
        prepare_kernel,
        out_shape=(
            pltpu.VMEM((size, size), f32),
            pltpu.VMEM((16, size), f32),
            pltpu.VMEM((groups, size, width), f32),
            pltpu.VMEM((groups, width), f32),
            pltpu.VMEM((slots, size, n), f32),
            pltpu.VMEM((slots, 8, n), f32),
        ),
        in_specs=[vmem] * 6,
        out_specs=[vmem] * 6,
        compiler_params=params,
        cost_estimate=pl.CostEstimate(flops=COST // 2, bytes_accessed=0, transcendentals=0),
        name="root_prepare",
    )(*local(owners, part, root_matrix, root_row, answers, solved))

    leaf_dir, node_dir, root_dir = pl.pallas_call(
        functools.partial(root_kernel, band),
        out_shape=(
            jax.ShapeDtypeStruct((slots, n), f32),
            jax.ShapeDtypeStruct((groups, band), f32),
            jax.ShapeDtypeStruct((1, size), f32),
        ),
        in_specs=[vmem] * (6 + len(others)),
        out_specs=(vmem, vmem, vmem),
        scratch_shapes=[
            pltpu.VMEM((size, size), f32),
            pltpu.VMEM((16, size), f32),
            pltpu.VMEM((size, 2 * size), f32),
        ],
        compiler_params=params,
        name="root_solve",
    )(*local(*prepared, *others))
    return leaf_dir, node_dir, root_dir[0]


def solution(mesh):
    return jax.shard_map(
        functools.partial(body, mesh.shape["leaf"], mesh.shape["grp"]),
        mesh=mesh,
        in_specs=(
            P(("leaf", "grp")),
            P(("leaf", "grp"), None, None),
            P(("leaf", "grp"), None, None),
            P(("leaf", "grp"), None),
            P("grp", "leaf", None),
            P("grp", "leaf", None),
            P("grp", "leaf"),
            P(),
            P(),
        ),
        out_specs=(P(("leaf", "grp"), None), P("grp", "leaf"), P()),
        check_vma=False,
    )
```

```python
import functools

import jax
import jax.numpy as jnp
from jax import lax
from jax.experimental import pallas as pl
from jax.experimental.pallas import tpu as pltpu
from jax.sharding import PartitionSpec as P

f32 = jnp.float32
bf16 = jnp.bfloat16
FLOOR = 0.1
STEPS = 5
ROOT_STEPS = 6
WARM_STEPS = 3
COST = 3_000_000_000
KERNEL_VMEM = 24 << 20
ACCEPT = 4e-5


def mul(a, b):
    return jnp.dot(a, b, preferred_element_type=f32)


def split(a):
    high = a.astype(bf16)
    return high, (a - high.astype(f32)).astype(bf16)


def split3(a):
    high = a.astype(bf16)
    rest = a - high.astype(f32)
    mid = rest.astype(bf16)
    return high, mid, (rest - mid.astype(f32)).astype(bf16)


def beside(*parts):
    return jnp.concatenate(parts, axis=1)


def above(*parts):
    return jnp.concatenate(parts, axis=0)


def mul3(a, b):
    ah, al = split(a)
    bh, bl = split(b)
    return mul(beside(ah, ah, al), above(bh, bl, bh))


def grid_of(rows, cols):
    return (
        lax.broadcasted_iota(jnp.int32, (rows, cols), 0),
        lax.broadcasted_iota(jnp.int32, (rows, cols), 1),
    )


def identity(n):
    row, col = grid_of(n, n)
    return (row == col).astype(f32)


def pack_symmetric(full, extra):
    n = full.shape[0]
    half = n // 2
    row, col = grid_of(half, n)
    lower = full[half:]
    moved = pltpu.roll(lower, half, 1)
    top = jnp.where(col < row, moved, full[:half])
    diagonal = jnp.sum(jnp.where(col == row + half, lower, 0.0), axis=0, keepdims=True)
    row8, _ = grid_of(8, n)
    tail = jnp.where(row8 == 0, jnp.broadcast_to(extra, (8, n)), 0.0)
    tail = jnp.where(row8 == 1, jnp.broadcast_to(diagonal, (8, n)), tail)
    return top, tail


def unpack_symmetric(top, diagonal):
    half, n = top.shape
    row, col = grid_of(half, n)
    flipped = jnp.concatenate([top, jnp.zeros_like(top)], axis=0).T
    upper = jnp.where((col < half) & (col < row), flipped[:half], top)
    inner = pltpu.roll(jnp.where(col < row, top, flipped[:half]), half, 1)
    inner = jnp.where(col == row + half, jnp.broadcast_to(diagonal, (half, n)), inner)
    lower = jnp.where(col < half, flipped[half:], inner)
    return jnp.concatenate([upper, lower], axis=0)


def coarse_inverse(bound, matrices, steps):
    one = identity(matrices[0].shape[0])
    alpha = 2.0 / (bound + FLOOR)
    delta = (bound - FLOOR) / (bound + FLOOR)
    square = delta * delta
    scale = 2.0 / (2.0 - square)
    scaled = [alpha * m for m in matrices]
    errors = [(one - s).astype(bf16) for s in scaled]
    inverses = [((scale * alpha) * (2.0 * one - s)).astype(bf16) for s in scaled]
    for _ in range(steps - 1):
        errors = [(scale * (mul(e, e) - (0.5 * square) * one)).astype(bf16) for e in errors]
        delta = square / (2.0 - square)
        square = delta * delta
        scale = 2.0 / (2.0 - square)
        inverses = [
            (scale * (v.astype(f32) + mul(e, v))).astype(bf16) for e, v in zip(errors, inverses)
        ]
    return inverses


def warm_inverse(matrix, near, low, steps):
    one = identity(matrix.shape[0])
    product = mul(near, matrix.astype(bf16))
    bound = jnp.maximum(norm_bound(product), 2.0 * low)
    alpha = 2.0 / (bound + low)
    delta = (bound - low) / (bound + low)
    square = delta * delta
    scale = 2.0 / (2.0 - square)
    error = (one - alpha * product).astype(bf16)
    inverse = (alpha * near.astype(f32)).astype(bf16)
    for step in range(steps):
        inverse = (scale * (inverse.astype(f32) + mul(error, inverse))).astype(bf16)
        if step + 1 < steps:
            error = (scale * (mul(error, error) - (0.5 * square) * one)).astype(bf16)
            delta = square / (2.0 - square)
            square = delta * delta
            scale = 2.0 / (2.0 - square)
    return inverse


def finish(matrices, inverses, rights):
    errors = [
        identity(m.shape[0]) - mul(beside(v, v, v), above(*split3(m)))
        for m, v in zip(matrices, inverses)
    ]
    pieces = [split(e) for e in errors]
    squares = [mul(h, h).astype(bf16) for h, _ in pieces]
    first = []
    for right, (eh, el) in zip(rights, pieces):
        rh, rl = split(right)
        first.append(right + mul(beside(rh, rh, rl), above(eh, el, eh)))
    second = [mul(z.astype(bf16), s) for z, s in zip(first, squares)]
    found = [
        mul(beside(*split3(z + d)), above(v, v, v)) for z, d, v in zip(first, second, inverses)
    ]
    return found, [misfits(d, z) for z, d in zip(first, second)]


def misfits(change, values):
    got = jnp.sum(change * change, axis=1, keepdims=True)
    allowed = ACCEPT * jnp.sum(values * values, axis=1, keepdims=True)
    return jnp.where(got <= allowed, 0.0, 1.0)


def eliminate(work):
    n, width = work.shape

    def step(k, carry):
        row, col = grid_of(8, width)
        base = pl.multiple_of((k // 8) * 8, 8)
        block = work[pl.ds(base, 8), :]
        pivot_row = jnp.sum(jnp.where(row == k - base, block, 0.0), axis=0, keepdims=True)
        pivot = jnp.sum(jnp.where(col[:1] == k, pivot_row, 0.0), axis=1, keepdims=True)
        scaled = pivot_row / pivot
        full = work[...]
        row, col = grid_of(n, width)
        column = jnp.sum(jnp.where(col == k, full, 0.0), axis=1, keepdims=True)
        work[...] = jnp.where(row == k, scaled, full - column * scaled)
        return carry

    lax.fori_loop(0, n, step, 0)


def solve_again(work, matrix, right):
    n, rows = matrix.shape[0], right.shape[0]
    work[:, :n] = matrix
    padded = above(right, jnp.zeros((work.shape[1] - n - rows, n), f32))
    work[:, n:] = padded.T
    eliminate(work)
    return work[:, n:].T[:rows]


def norm_bound(*matrices):
    sums = [jnp.sum(jnp.abs(m), axis=0, keepdims=True) for m in matrices]
    most = sums[0]
    for other in sums[1:]:
        most = jnp.maximum(most, other)
    return jnp.max(most, axis=1, keepdims=True)


def stage_kernel(parent, matrix, link, rhs, *refs):
    matrix_rows, link_rows, rhs_rows, sems = refs[-4:]
    count = (len(refs) - 6) // 2
    rest, owners, own, targets = refs[:count], refs[count], refs[count + 1], refs[count + 2 : -4]
    pairs = ((matrix, matrix_rows), (link, link_rows), (rhs, rhs_rows), *zip(rest, targets))
    copies = [
        pltpu.make_async_copy(source, target, sems.at[i])
        for i, (source, target) in enumerate(pairs)
    ]
    for copy in copies:
        copy.start()
    for s in range(owners.shape[0]):
        owners[s] = jnp.full(owners.shape[1:], parent[s].astype(f32))
    groups, band, _ = matrix_rows.shape
    rows = groups * band
    own[0, 2 * rows :, :] = jnp.zeros((groups, own.shape[2]), f32)
    for copy in copies[:3]:
        copy.wait()
    for q in range(groups):
        own[0, q * band : (q + 1) * band, :] = matrix_rows[q]
        own[0, rows + q * band : rows + (q + 1) * band, :] = link_rows[q]
    own[0, 2 * rows :, :band] = rhs_rows[...]
    for copy in copies[3:]:
        copy.wait()


def invert_kernel(matrix, inverse):
    for s in range(matrix.shape[0]):
        block = matrix[s]
        inverse[s] = coarse_inverse(norm_bound(block), [block], STEPS)[0]


def leaf_kernel(owners, matrix, coupling, residual, inverse, solved, message, work):
    n = matrix.shape[1]
    width = coupling.shape[2]
    for s in range(matrix.shape[0]):
        right = above(coupling[s].T, jnp.broadcast_to(residual[s : s + 1, :], (16, n)))
        found, bad = finish([matrix[s]], [inverse[s]], [right])
        solved[s] = found[0]

        @pl.when(jnp.sum(bad[0]) > 0.0)
        def _():
            right = above(coupling[s].T, jnp.broadcast_to(residual[s : s + 1, :], (16, n)))
            solved[s] = solve_again(work, matrix[s], right)

        product = mul3(solved[s], coupling[s])
        top, tail = pack_symmetric(product[:width], product[width : width + 1])
        row8, _ = grid_of(8, width)
        tail = jnp.where(row8 == 2, owners[s], tail)
        message[s, : width // 2, :] = top
        message[s, width // 2 :, :] = tail


def assemble_kernel(sources, groups, band, *refs):
    data = refs[:-3]
    full, links, shift = refs[-3:]
    rows = groups * band
    here = lax.axis_index("leaf") if len(sources) > 1 else 0
    at = 0
    total = None
    for piece in data:
        for j in range(piece.shape[0]):
            place = pl.multiple_of((here ^ sources[at]) * band, band) if len(sources) > 1 else 0
            at += 1
            for q in range(groups):
                full[q, pl.ds(place, band), :] = piece[j, q * band : (q + 1) * band, :]
                links[q, pl.ds(place, band), :] = piece[j, rows + q * band : rows + (q + 1) * band, :]
            last = piece[j, 2 * rows :, :]
            if len(sources) > 1:
                last = pltpu.roll(last, place, 1)
            total = last if total is None else total + last
    shift[...] = total


def add_messages(sums, messages):
    if not messages:
        return sums
    row = messages[0].shape[1] - 6
    for piece in messages:
        for j in range(piece.shape[0]):
            message = piece[j]
            owner = message[row : row + 1, :]
            sums = [x + jnp.where(owner == q, message, 0.0) for q, x in enumerate(sums)]
    return sums


def sum_kernel(*refs):
    sums = refs[-1]
    groups = sums.shape[0]
    zero = jnp.zeros(sums.shape[1:], f32)
    for q, total in enumerate(add_messages([zero] * groups, refs[:-1])):
        sums[q] = total


def node_kernel(regular, links, shift, partial, *refs):
    messages = refs[:-5]
    answers, message, full, rights, work = refs[-5:]
    groups, n, width = links.shape
    half = n // 2
    sums = add_messages([partial[q] for q in range(groups)], messages)
    tops = [x[:half] for x in sums]
    tails = [x[half:] for x in sums]
    for q in range(groups):
        full[q] = regular[q] + unpack_symmetric(tops[q], tails[q][1:2])
        rights[q, :width] = links[q].T
        rights[q, width:] = jnp.broadcast_to(tails[q][:1] - shift[q : q + 1], (16, n))
    blocks = [full[q] for q in range(groups)]
    inverses = coarse_inverse(norm_bound(*blocks), blocks, STEPS)
    found, bad = finish(blocks, inverses, [rights[q] for q in range(groups)])
    for q in range(groups):
        answers[q] = found[q]

    @pl.when(jnp.sum(sum(bad)) > 0.0)
    def _():
        for q in range(groups):
            answers[q] = solve_again(work, full[q], rights[q])

    total = None
    for q in range(groups):
        part = mul3(answers[q], links[q])
        total = part if q == 0 else total + part
    top, tail = pack_symmetric(total[:width], total[width : width + 1])
    message[: width // 2, :] = top
    message[width // 2 :, :] = tail


def prepare_kernel(
    sets, owners, part, matrix, rhs, answers, solved, base, base_row, near, moves, fixed, leaf_moves, leaf_fixed
):
    size = matrix.shape[0]
    half = size // 2
    groups, _, n = answers.shape
    mine = unpack_symmetric(part[:half, :], part[half + 1 : half + 2, :])
    base[...] = matrix[...] + mine
    guess = matrix[...] + sets * mine
    near[...] = coarse_inverse(norm_bound(guess), [guess], ROOT_STEPS)[0]
    base_row[...] = jnp.broadcast_to(rhs[...] - part[half : half + 1, :], base_row.shape)
    for q in range(groups):
        fixed[q : q + 1, :] = answers[q, size : size + 1, :]
        moves[q] = answers[q, :size, :]
    for s in range(solved.shape[0]):
        owner = owners[s, :1, :1]
        own = jnp.zeros_like(answers[0])
        for q in range(groups):
            own = jnp.where(owner == q, answers[q], own)
        product = mul3(own, solved[s, :n, :])
        live = owner >= 0.0
        leaf_moves[s] = jnp.where(live, -product[:size], 0.0)
        last = solved[s, n : n + 8, :] - product[size : size + 8]
        leaf_fixed[s] = jnp.where(live, last, 0.0)


def root_kernel(
    sets, band, base, base_row, near, moves, fixed, leaf_moves, leaf_fixed, *refs
):
    others = refs[:-6]
    leaf_dir, node_dir, root_dir, full, found_root, work = refs[-6:]
    size = base.shape[0]
    half = size // 2
    groups, _, n = moves.shape
    system = base[...]
    right = base_row[...]
    for other in others:
        system = system + unpack_symmetric(other[:half, :], other[half + 1 : half + 2, :])
        right = right - other[half : half + 1, :]
    full[...] = system
    inverse = warm_inverse(system, near[...], 1.0 / sets, WARM_STEPS)
    found, bad = finish([system], [inverse], [right])
    found_root[...] = found[0]

    @pl.when(jnp.sum(bad[0]) > 0.0)
    def _():
        found_root[...] = solve_again(work, full[...], right)

    answer = found_root[:1, :]
    root_dir[...] = answer
    column = jnp.broadcast_to(answer, (size, size)).T
    each = [jnp.sum(column * moves[q], axis=0, keepdims=True) for q in range(groups)]
    every = above(*each) + fixed[...]
    if band == n:
        node_dir[...] = every
    else:
        me = lax.axis_index("leaf")
        node_dir[...] = pltpu.roll(every, lax.rem(n - me * band, n), 1)[:, :band]
    wide = leaf_moves.shape[2] // size
    for s in range(leaf_moves.shape[0]):
        terms = beside(*[column] * wide) * leaf_moves[s]
        leaf_dir[s : s + 1, :] = jnp.sum(terms, axis=0, keepdims=True) + leaf_fixed[s, :1, :]


def gather_steps(extent):
    steps = []
    while extent > 1:
        extent //= 2
        steps.append(extent)
    return steps


def moved(values, axis, extent, distance):
    return lax.ppermute(values, axis, [(i, i ^ distance) for i in range(extent)])


def exchange(pieces, axis, extent, distance):
    sent = pieces[0] if len(pieces) == 1 else jnp.concatenate(pieces, axis=0)
    pieces.append(moved(sent, axis, extent, distance))


def doubled(values, axis, extent):
    pieces = [values]
    for distance in gather_steps(extent):
        exchange(pieces, axis, extent, distance)
    return pieces


def hold(pieces, value):
    pieces[-1] = lax.optimization_barrier((value, pieces[-1]))[1]


def source_offsets(steps):
    offsets = [0]
    for distance in steps:
        offsets = offsets + [o ^ distance for o in offsets]
    return tuple(offsets)


def other_parts(values, axis, extent):
    if extent == 1:
        return []
    if extent & (extent - 1):
        return [lax.psum(values, axis) - values]
    steps = gather_steps(extent)
    pieces = []
    for distance in reversed(steps):
        pieces.append(moved(values, axis, extent, distance))
        values = values + pieces[-1]
    return pieces


def remote(*values):
    return [pltpu.with_memory_space_constraint(v, pltpu.HBM) for v in values]


def local(*values):
    return [pltpu.with_memory_space_constraint(v, pltpu.VMEM) for v in values]


def body(
    leaves,
    sets,
    slot_parent,
    leaf_matrix,
    coupling,
    leaf_residual_rows,
    node_matrix,
    node_link,
    node_rhs,
    root_matrix,
    root_rhs,
):
    slots, n = leaf_residual_rows.shape
    groups, band, width = node_matrix.shape
    size = node_link.shape[2]
    doubling = leaves & (leaves - 1) == 0
    vmem = pl.BlockSpec(memory_space=pltpu.VMEM)
    smem = pl.BlockSpec(memory_space=pltpu.SMEM)
    params = pltpu.CompilerParams(vmem_limit_bytes=KERNEL_VMEM)

    paced = doubling and band % 8 == 0
    hbm = pl.BlockSpec(memory_space=pltpu.HBM)
    nodes = [node_matrix, node_link, node_rhs]
    staged = [leaf_matrix, coupling, leaf_residual_rows, root_matrix, root_rhs[None, :]]
    owners, own, *near, root_matrix, root_row = pl.pallas_call(
        stage_kernel,
        out_shape=(
            pltpu.VMEM((slots, 8, width), f32),
            pltpu.VMEM((1, 2 * groups * band + groups, width), f32),
            *[pltpu.VMEM(a.shape, f32) for a in staged],
        ),
        in_specs=[smem] + [hbm] * (3 + len(staged)),
        out_specs=[vmem] * (2 + len(staged)),
        scratch_shapes=[pltpu.VMEM(a.shape, f32) for a in nodes]
        + [pltpu.SemaphoreType.DMA((3 + len(staged),))],
        compiler_params=params,
        name="stage",
    )(slot_parent, *remote(*nodes, *staged))
    def invert():
        return pl.pallas_call(
            invert_kernel,
            out_shape=pltpu.VMEM((slots, n, n), bf16),
            in_specs=[vmem],
            out_specs=vmem,
            compiler_params=params,
            cost_estimate=pl.CostEstimate(flops=COST, bytes_accessed=0, transcendentals=0),
            name="leaf_invert",
        )(*local(near[0]))

    def solve(matrix, coupling, residual, inverse):
        return pl.pallas_call(
            leaf_kernel,
            out_shape=(
                pltpu.VMEM((slots, width + 16, n), f32),
                pltpu.VMEM((slots, width // 2 + 8, width), f32),
            ),
            in_specs=[vmem] * 5,
            out_specs=(vmem, vmem),
            scratch_shapes=[
                pltpu.VMEM((n, n + 2 * width), f32),
            ],
            compiler_params=params,
            cost_estimate=pl.CostEstimate(flops=COST, bytes_accessed=0, transcendentals=0),
            name="leaf_solve",
        )(*local(owners, matrix, coupling, residual, inverse))

    if paced:
        data = [own]
        held = band
        order = [8, 4, 2, 1]
        sources = source_offsets(order)
        exchange(data, "leaf", leaves, 8)
        inverse = invert()
        hold(data, inverse)
        exchange(data, "leaf", leaves, 4)
        solved, message = solve(*near, inverse)
        messages = [message]
        exchange(messages, "leaf", leaves, 2)
        hold(data, messages[-1])
        exchange(data, "leaf", leaves, 2)
        exchange(messages, "leaf", leaves, 8)
        exchange(messages, "leaf", leaves, 4)
        hold(data, messages[-1])
        exchange(messages, "leaf", leaves, 1)
        exchange(data, "leaf", leaves, 1)
    else:
        rank = lax.axis_index("leaf")
        placed = lax.dynamic_update_slice(
            jnp.zeros((groups, width), f32), node_rhs, (jnp.zeros((), jnp.int32), rank * band)
        )
        every = lax.all_gather(
            jnp.concatenate([node_matrix, node_link], axis=0), "leaf", axis=1, tiled=True
        )
        data = [
            jnp.concatenate([every.reshape(-1, width), lax.psum(placed, "leaf")], axis=0)[None]
        ]
        held = width
        sources = (0,)

        inverse = invert()
        solved, message = solve(*near, inverse)
        if doubling:
            messages = doubled(message, "leaf", leaves)
        else:
            messages = [lax.all_gather(message, "leaf", axis=0, tiled=True)]

    node_blocks = pl.pallas_call(
        functools.partial(assemble_kernel, sources, groups, held),
        out_shape=(
            pltpu.VMEM((groups, width, width), f32),
            pltpu.VMEM((groups, width, size), f32),
            pltpu.VMEM((groups, width), f32),
        ),
        in_specs=[vmem] * len(data),
        out_specs=(vmem, vmem, vmem),
        compiler_params=params,
        name="node_assemble",
    )(*local(*data))

    early = messages[:-1] or messages
    partial = pl.pallas_call(
        sum_kernel,
        out_shape=pltpu.VMEM((groups, width // 2 + 8, width), f32),
        in_specs=[vmem] * len(early),
        out_specs=vmem,
        compiler_params=params,
        cost_estimate=pl.CostEstimate(flops=COST // 4, bytes_accessed=0, transcendentals=0),
        name="node_sum",
    )(*local(*early))
    late = messages[len(early) :]

    answers, part = pl.pallas_call(
        node_kernel,
        out_shape=(
            pltpu.VMEM((groups, size + 16, width), f32),
            pltpu.VMEM((size // 2 + 8, size), f32),
        ),
        in_specs=[vmem] * (4 + len(late)),
        out_specs=(vmem, vmem),
        scratch_shapes=[
            pltpu.VMEM((groups, width, width), f32),
            pltpu.VMEM((groups, size + 16, width), f32),
            pltpu.VMEM((width, width + 2 * size), f32),
        ],
        compiler_params=params,
        name="node_solve",
    )(*local(*node_blocks, partial, *late))

    others = other_parts(part, "grp", sets)
    prepared = pl.pallas_call(
        functools.partial(prepare_kernel, sets),
        out_shape=(
            pltpu.VMEM((size, size), f32),
            pltpu.VMEM((16, size), f32),
            pltpu.VMEM((size, size), bf16),
            pltpu.VMEM((groups, size, width), f32),
            pltpu.VMEM((groups, width), f32),
            pltpu.VMEM((slots, size, n), f32),
            pltpu.VMEM((slots, 8, n), f32),
        ),
        in_specs=[vmem] * 6,
        out_specs=[vmem] * 7,
        compiler_params=params,
        cost_estimate=pl.CostEstimate(flops=COST // 2, bytes_accessed=0, transcendentals=0),
        name="root_prepare",
    )(*local(owners, part, root_matrix, root_row, answers, solved))

    leaf_dir, node_dir, root_dir = pl.pallas_call(
        functools.partial(root_kernel, sets, band),
        out_shape=(
            jax.ShapeDtypeStruct((slots, n), f32),
            jax.ShapeDtypeStruct((groups, band), f32),
            jax.ShapeDtypeStruct((1, size), f32),
        ),
        in_specs=[vmem] * (7 + len(others)),
        out_specs=(vmem, vmem, vmem),
        scratch_shapes=[
            pltpu.VMEM((size, size), f32),
            pltpu.VMEM((16, size), f32),
            pltpu.VMEM((size, 2 * size), f32),
        ],
        compiler_params=params,
        name="root_solve",
    )(*local(*prepared, *others))
    return leaf_dir, node_dir, root_dir[0]


def solution(mesh):
    return jax.shard_map(
        functools.partial(body, mesh.shape["leaf"], mesh.shape["grp"]),
        mesh=mesh,
        in_specs=(
            P(("leaf", "grp")),
            P(("leaf", "grp"), None, None),
            P(("leaf", "grp"), None, None),
            P(("leaf", "grp"), None),
            P("grp", "leaf", None),
            P("grp", "leaf", None),
            P("grp", "leaf"),
            P(),
            P(),
        ),
        out_specs=(P(("leaf", "grp"), None), P("grp", "leaf"), P()),
        check_vma=False,
    )
```

```python
import functools

import jax
import jax.numpy as jnp
from jax import lax
from jax.experimental import pallas as pl
from jax.experimental.pallas import tpu as pltpu
from jax.sharding import PartitionSpec as P

f32 = jnp.float32
bf16 = jnp.bfloat16
FLOOR = 0.1
STEPS = 5
ROOT_STEPS = 6
WARM_STEPS = 3
COST = 3_000_000_000
KERNEL_VMEM = 24 << 20
ACCEPT = 4e-5


def mul(a, b):
    return jnp.dot(a, b, preferred_element_type=f32)


def split(a):
    high = a.astype(bf16)
    return high, (a - high.astype(f32)).astype(bf16)


def split3(a):
    high = a.astype(bf16)
    rest = a - high.astype(f32)
    mid = rest.astype(bf16)
    return high, mid, (rest - mid.astype(f32)).astype(bf16)


def beside(*parts):
    return jnp.concatenate(parts, axis=1)


def above(*parts):
    return jnp.concatenate(parts, axis=0)


def mul3(a, b):
    ah, al = split(a)
    bh, bl = split(b)
    return mul(beside(ah, ah, al), above(bh, bl, bh))


def grid_of(rows, cols):
    return (
        lax.broadcasted_iota(jnp.int32, (rows, cols), 0),
        lax.broadcasted_iota(jnp.int32, (rows, cols), 1),
    )


def identity(n):
    row, col = grid_of(n, n)
    return (row == col).astype(f32)


def pack_symmetric(full, extra):
    n = full.shape[0]
    half = n // 2
    row, col = grid_of(half, n)
    lower = full[half:]
    moved = pltpu.roll(lower, half, 1)
    top = jnp.where(col < row, moved, full[:half])
    diagonal = jnp.sum(jnp.where(col == row + half, lower, 0.0), axis=0, keepdims=True)
    row8, _ = grid_of(8, n)
    tail = jnp.where(row8 == 0, jnp.broadcast_to(extra, (8, n)), 0.0)
    tail = jnp.where(row8 == 1, jnp.broadcast_to(diagonal, (8, n)), tail)
    return top, tail


def unpack_symmetric(top, diagonal):
    half, n = top.shape
    row, col = grid_of(half, n)
    flipped = jnp.concatenate([top, jnp.zeros_like(top)], axis=0).T
    upper = jnp.where((col < half) & (col < row), flipped[:half], top)
    inner = pltpu.roll(jnp.where(col < row, top, flipped[:half]), half, 1)
    inner = jnp.where(col == row + half, jnp.broadcast_to(diagonal, (half, n)), inner)
    lower = jnp.where(col < half, flipped[half:], inner)
    return jnp.concatenate([upper, lower], axis=0)


def coarse_inverse(bound, matrices, steps):
    one = identity(matrices[0].shape[0])
    alpha = 2.0 / (bound + FLOOR)
    delta = (bound - FLOOR) / (bound + FLOOR)
    square = delta * delta
    scale = 2.0 / (2.0 - square)
    scaled = [alpha * m for m in matrices]
    errors = [(one - s).astype(bf16) for s in scaled]
    inverses = [((scale * alpha) * (2.0 * one - s)).astype(bf16) for s in scaled]
    for _ in range(steps - 1):
        errors = [(scale * (mul(e, e) - (0.5 * square) * one)).astype(bf16) for e in errors]
        delta = square / (2.0 - square)
        square = delta * delta
        scale = 2.0 / (2.0 - square)
        inverses = [
            (scale * (v.astype(f32) + mul(e, v))).astype(bf16) for e, v in zip(errors, inverses)
        ]
    return inverses


def warm_inverse(matrix, near, low, steps):
    one = identity(matrix.shape[0])
    product = mul(near, matrix.astype(bf16))
    bound = jnp.maximum(norm_bound(product), 2.0 * low)
    alpha = 2.0 / (bound + low)
    delta = (bound - low) / (bound + low)
    square = delta * delta
    scale = 2.0 / (2.0 - square)
    error = (one - alpha * product).astype(bf16)
    inverse = (alpha * near.astype(f32)).astype(bf16)
    for step in range(steps):
        inverse = (scale * (inverse.astype(f32) + mul(error, inverse))).astype(bf16)
        if step + 1 < steps:
            error = (scale * (mul(error, error) - (0.5 * square) * one)).astype(bf16)
            delta = square / (2.0 - square)
            square = delta * delta
            scale = 2.0 / (2.0 - square)
    return inverse


def finish(matrices, inverses, rights):
    errors = [
        identity(m.shape[0]) - mul(beside(v, v), above(*split(m)))
        for m, v in zip(matrices, inverses)
    ]
    pieces = [split(e) for e in errors]
    squares = [mul(h, h).astype(bf16) for h, _ in pieces]
    first = []
    for right, (eh, el) in zip(rights, pieces):
        rh, rl = split(right)
        first.append(right + mul(beside(rh, rh, rl), above(eh, el, eh)))
    second = [mul(z.astype(bf16), s) for z, s in zip(first, squares)]
    found = [
        mul(beside(*split(z + d)), above(v, v)) for z, d, v in zip(first, second, inverses)
    ]
    return found, [misfits(d, z) for z, d in zip(first, second)]


def misfits(change, values):
    got = jnp.sum(change * change, axis=1, keepdims=True)
    allowed = ACCEPT * jnp.sum(values * values, axis=1, keepdims=True)
    return jnp.where(got <= allowed, 0.0, 1.0)


def eliminate(work):
    n, width = work.shape

    def step(k, carry):
        row, col = grid_of(8, width)
        base = pl.multiple_of((k // 8) * 8, 8)
        block = work[pl.ds(base, 8), :]
        pivot_row = jnp.sum(jnp.where(row == k - base, block, 0.0), axis=0, keepdims=True)
        pivot = jnp.sum(jnp.where(col[:1] == k, pivot_row, 0.0), axis=1, keepdims=True)
        scaled = pivot_row / pivot
        full = work[...]
        row, col = grid_of(n, width)
        column = jnp.sum(jnp.where(col == k, full, 0.0), axis=1, keepdims=True)
        work[...] = jnp.where(row == k, scaled, full - column * scaled)
        return carry

    lax.fori_loop(0, n, step, 0)


def solve_again(work, matrix, right):
    n, rows = matrix.shape[0], right.shape[0]
    work[:, :n] = matrix
    padded = above(right, jnp.zeros((work.shape[1] - n - rows, n), f32))
    work[:, n:] = padded.T
    eliminate(work)
    return work[:, n:].T[:rows]


def norm_bound(*matrices):
    sums = [jnp.sum(jnp.abs(m), axis=0, keepdims=True) for m in matrices]
    most = sums[0]
    for other in sums[1:]:
        most = jnp.maximum(most, other)
    return jnp.max(most, axis=1, keepdims=True)


def stage_kernel(parent, matrix, link, rhs, *refs):
    matrix_rows, link_rows, rhs_rows, sems = refs[-4:]
    count = (len(refs) - 6) // 2
    rest, owners, own, targets = refs[:count], refs[count], refs[count + 1], refs[count + 2 : -4]
    pairs = ((matrix, matrix_rows), (link, link_rows), (rhs, rhs_rows), *zip(rest, targets))
    copies = [
        pltpu.make_async_copy(source, target, sems.at[i])
        for i, (source, target) in enumerate(pairs)
    ]
    for copy in copies:
        copy.start()
    for s in range(owners.shape[0]):
        owners[s] = jnp.full(owners.shape[1:], parent[s].astype(f32))
    groups, band, _ = matrix_rows.shape
    rows = groups * band
    own[0, 2 * rows :, :] = jnp.zeros((groups, own.shape[2]), f32)
    for copy in copies[:3]:
        copy.wait()
    for q in range(groups):
        own[0, q * band : (q + 1) * band, :] = matrix_rows[q]
        own[0, rows + q * band : rows + (q + 1) * band, :] = link_rows[q]
    own[0, 2 * rows :, :band] = rhs_rows[...]
    for copy in copies[3:]:
        copy.wait()


def invert_kernel(matrix, inverse):
    for s in range(matrix.shape[0]):
        block = matrix[s]
        inverse[s] = coarse_inverse(norm_bound(block), [block], STEPS)[0]


def leaf_kernel(owners, matrix, coupling, residual, inverse, solved, message, work):
    n = matrix.shape[1]
    width = coupling.shape[2]
    for s in range(matrix.shape[0]):
        right = above(coupling[s].T, jnp.broadcast_to(residual[s : s + 1, :], (16, n)))
        found, bad = finish([matrix[s]], [inverse[s]], [right])
        solved[s] = found[0]

        @pl.when(jnp.sum(bad[0]) > 0.0)
        def _():
            right = above(coupling[s].T, jnp.broadcast_to(residual[s : s + 1, :], (16, n)))
            solved[s] = solve_again(work, matrix[s], right)

        product = mul3(solved[s], coupling[s])
        top, tail = pack_symmetric(product[:width], product[width : width + 1])
        row8, _ = grid_of(8, width)
        tail = jnp.where(row8 == 2, owners[s], tail)
        message[s, : width // 2, :] = top
        message[s, width // 2 :, :] = tail


def pack_kernel(leaves, own, other, packed):
    n = own.shape[2]
    half = n // 2
    band = half // (leaves // 2)
    groups = own.shape[1] // (2 * band + 1)
    rows = groups * band
    here = lax.axis_index("leaf")
    is_top = here < leaves // 2
    place = lax.rem(here, leaves // 2) * band
    top = jnp.where(is_top, own[0], other[0])
    low = jnp.where(is_top, other[0], own[0])
    row, col = grid_of(band, n)
    row = row + place
    diagonals = []
    for q in range(groups):
        at = slice(q * band, (q + 1) * band)
        packed[0, at, :] = jnp.where(col < row, pltpu.roll(low[at], half, 1), top[at])
        diagonals.append(
            jnp.sum(jnp.where(col == row + half, low[at], 0.0), axis=0, keepdims=True)
        )
    packed[0, rows : 2 * rows, :] = top[rows : 2 * rows]
    packed[0, 2 * rows : 3 * rows, :] = low[rows : 2 * rows]
    _, col = grid_of(groups, n)
    diagonal = pltpu.roll(above(*diagonals), lax.rem(half + 2 * band - place, n), 1)
    last = jnp.where(col < 2 * band, pltpu.roll(low[2 * rows :], band, 1), diagonal)
    last = jnp.where(col < band, top[2 * rows :], last)
    packed[0, 3 * rows :, :] = jnp.where(col < 3 * band, last, 0.0)


def assemble_kernel(leaves, sources, groups, band, *refs):
    data = refs[:-2]
    regular, links = refs[-2:]
    n = regular.shape[2]
    half = n // 2
    rows = groups * band
    here = lax.axis_index("leaf")
    row, col = grid_of(groups, n)
    at = 0
    shift = jnp.zeros((groups, n), f32)
    diagonal = jnp.zeros((groups, n), f32)
    for piece in data:
        for j in range(piece.shape[0]):
            place = lax.rem(here ^ sources[at], leaves // 2) * band
            place = pl.multiple_of(place, band)
            at += 1
            for q in range(groups):
                regular[q, pl.ds(place, band), :] = piece[j, q * band : (q + 1) * band, :]
                start = rows + q * band
                links[q, pl.ds(place, band), :] = piece[j, start : start + band, :]
                start = start + rows
                links[q, pl.ds(half + place, band), :] = piece[j, start : start + band, :]
            last = piece[j, 3 * rows :, :]
            first = jnp.where(col < band, last, 0.0)
            second = jnp.where((col >= band) & (col < 2 * band), last, 0.0)
            third = jnp.where(col >= 2 * band, last, 0.0)
            shift = shift + pltpu.roll(first, place, 1)
            shift = shift + pltpu.roll(second, lax.rem(half + place - band + n, n), 1)
            diagonal = diagonal + pltpu.roll(third, lax.rem(half + place - 2 * band + n, n), 1)
    row8, _ = grid_of(8, n)
    for q in range(groups):
        tail = jnp.where(row8 == 0, -shift[q : q + 1], 0.0)
        regular[q, half:, :] = jnp.where(row8 == 1, diagonal[q : q + 1], tail)


def add_messages(sums, messages):
    if not messages:
        return sums
    row = messages[0].shape[1] - 6
    for piece in messages:
        for j in range(piece.shape[0]):
            message = piece[j]
            owner = message[row : row + 1, :]
            sums = [x + jnp.where(owner == q, message, 0.0) for q, x in enumerate(sums)]
    return sums


def sum_kernel(*refs):
    sums = refs[-1]
    groups = sums.shape[0]
    zero = jnp.zeros(sums.shape[1:], f32)
    for q, total in enumerate(add_messages([zero] * groups, refs[:-1])):
        sums[q] = total


def node_kernel(regular, links, partial, *refs):
    messages = refs[:-5]
    answers, message, full, rights, work = refs[-5:]
    groups, n, width = links.shape
    half = n // 2
    sums = add_messages([regular[q] + partial[q] for q in range(groups)], messages)
    tops = [x[:half] for x in sums]
    tails = [x[half:] for x in sums]
    for q in range(groups):
        full[q] = unpack_symmetric(tops[q], tails[q][1:2])
        rights[q, :width] = links[q].T
        rights[q, width:] = jnp.broadcast_to(tails[q][:1], (16, n))
    blocks = [full[q] for q in range(groups)]
    inverses = coarse_inverse(norm_bound(*blocks), blocks, STEPS)
    found, bad = finish(blocks, inverses, [rights[q] for q in range(groups)])
    for q in range(groups):
        answers[q] = found[q]

    @pl.when(jnp.sum(sum(bad)) > 0.0)
    def _():
        for q in range(groups):
            answers[q] = solve_again(work, full[q], rights[q])

    total = None
    for q in range(groups):
        part = mul3(answers[q], links[q])
        total = part if q == 0 else total + part
    top, tail = pack_symmetric(total[:width], total[width : width + 1])
    message[: width // 2, :] = top
    message[width // 2 :, :] = tail


def prepare_kernel(
    sets, owners, part, matrix, rhs, answers, solved, base, base_row, near, moves, fixed, leaf_moves, leaf_fixed
):
    size = matrix.shape[0]
    half = size // 2
    groups, _, n = answers.shape
    mine = unpack_symmetric(part[:half, :], part[half + 1 : half + 2, :])
    base[...] = matrix[...] + mine
    guess = matrix[...] + sets * mine
    near[...] = coarse_inverse(norm_bound(guess), [guess], ROOT_STEPS)[0]
    base_row[...] = jnp.broadcast_to(rhs[...] - part[half : half + 1, :], base_row.shape)
    for q in range(groups):
        fixed[q : q + 1, :] = answers[q, size : size + 1, :]
        moves[q] = answers[q, :size, :]
    for s in range(solved.shape[0]):
        owner = owners[s, :1, :1]
        own = jnp.zeros_like(answers[0])
        for q in range(groups):
            own = jnp.where(owner == q, answers[q], own)
        product = mul3(own, solved[s, :n, :])
        live = owner >= 0.0
        leaf_moves[s] = jnp.where(live, -product[:size], 0.0)
        last = solved[s, n : n + 8, :] - product[size : size + 8]
        leaf_fixed[s] = jnp.where(live, last, 0.0)


def root_kernel(
    sets, band, base, base_row, near, moves, fixed, leaf_moves, leaf_fixed, *refs
):
    others = refs[:-6]
    leaf_dir, node_dir, root_dir, full, found_root, work = refs[-6:]
    size = base.shape[0]
    half = size // 2
    groups, _, n = moves.shape
    system = base[...]
    right = base_row[...]
    for other in others:
        system = system + unpack_symmetric(other[:half, :], other[half + 1 : half + 2, :])
        right = right - other[half : half + 1, :]
    full[...] = system
    inverse = warm_inverse(system, near[...], 1.0 / sets, WARM_STEPS)
    found, bad = finish([system], [inverse], [right])
    found_root[...] = found[0]

    @pl.when(jnp.sum(bad[0]) > 0.0)
    def _():
        found_root[...] = solve_again(work, full[...], right)

    answer = found_root[:1, :]
    root_dir[...] = answer
    column = jnp.broadcast_to(answer, (size, size)).T
    each = [jnp.sum(column * moves[q], axis=0, keepdims=True) for q in range(groups)]
    every = above(*each) + fixed[...]
    if band == n:
        node_dir[...] = every
    else:
        me = lax.axis_index("leaf")
        node_dir[...] = pltpu.roll(every, lax.rem(n - me * band, n), 1)[:, :band]
    wide = leaf_moves.shape[2] // size
    for s in range(leaf_moves.shape[0]):
        terms = beside(*[column] * wide) * leaf_moves[s]
        leaf_dir[s : s + 1, :] = jnp.sum(terms, axis=0, keepdims=True) + leaf_fixed[s, :1, :]


def gather_steps(extent):
    steps = []
    while extent > 1:
        extent //= 2
        steps.append(extent)
    return steps


def moved(values, axis, extent, distance):
    return lax.ppermute(values, axis, [(i, i ^ distance) for i in range(extent)])


def exchange(pieces, axis, extent, distance):
    sent = pieces[0] if len(pieces) == 1 else jnp.concatenate(pieces, axis=0)
    pieces.append(moved(sent, axis, extent, distance))


def doubled(values, axis, extent):
    pieces = [values]
    for distance in gather_steps(extent):
        exchange(pieces, axis, extent, distance)
    return pieces


def hold(pieces, value):
    pieces[-1] = lax.optimization_barrier((value, pieces[-1]))[1]


def source_offsets(steps):
    offsets = [0]
    for distance in steps:
        offsets = offsets + [o ^ distance for o in offsets]
    return tuple(offsets)


def other_parts(values, axis, extent):
    if extent == 1:
        return []
    if extent & (extent - 1):
        return [lax.psum(values, axis) - values]
    steps = gather_steps(extent)
    pieces = []
    for distance in reversed(steps):
        pieces.append(moved(values, axis, extent, distance))
        values = values + pieces[-1]
    return pieces


def remote(*values):
    return [pltpu.with_memory_space_constraint(v, pltpu.HBM) for v in values]


def local(*values):
    return [pltpu.with_memory_space_constraint(v, pltpu.VMEM) for v in values]


def body(
    leaves,
    sets,
    slot_parent,
    leaf_matrix,
    coupling,
    leaf_residual_rows,
    node_matrix,
    node_link,
    node_rhs,
    root_matrix,
    root_rhs,
):
    slots, n = leaf_residual_rows.shape
    groups, band, width = node_matrix.shape
    size = node_link.shape[2]
    doubling = leaves & (leaves - 1) == 0
    vmem = pl.BlockSpec(memory_space=pltpu.VMEM)
    smem = pl.BlockSpec(memory_space=pltpu.SMEM)
    params = pltpu.CompilerParams(vmem_limit_bytes=KERNEL_VMEM)

    paced = doubling and band % 8 == 0 and 4 <= leaves and 3 * band <= width
    hbm = pl.BlockSpec(memory_space=pltpu.HBM)
    nodes = [node_matrix, node_link, node_rhs]
    staged = [leaf_matrix, coupling, leaf_residual_rows, root_matrix, root_rhs[None, :]]
    owners, own, *near, root_matrix, root_row = pl.pallas_call(
        stage_kernel,
        out_shape=(
            pltpu.VMEM((slots, 8, width), f32),
            pltpu.VMEM((1, 2 * groups * band + groups, width), f32),
            *[pltpu.VMEM(a.shape, f32) for a in staged],
        ),
        in_specs=[smem] + [hbm] * (3 + len(staged)),
        out_specs=[vmem] * (2 + len(staged)),
        scratch_shapes=[pltpu.VMEM(a.shape, f32) for a in nodes]
        + [pltpu.SemaphoreType.DMA((3 + len(staged),))],
        compiler_params=params,
        name="stage",
    )(slot_parent, *remote(*nodes, *staged))
    def invert():
        return pl.pallas_call(
            invert_kernel,
            out_shape=pltpu.VMEM((slots, n, n), bf16),
            in_specs=[vmem],
            out_specs=vmem,
            compiler_params=params,
            cost_estimate=pl.CostEstimate(flops=COST, bytes_accessed=0, transcendentals=0),
            name="leaf_invert",
        )(*local(near[0]))

    def solve(matrix, coupling, residual, inverse):
        return pl.pallas_call(
            leaf_kernel,
            out_shape=(
                pltpu.VMEM((slots, width + 16, n), f32),
                pltpu.VMEM((slots, width // 2 + 8, width), f32),
            ),
            in_specs=[vmem] * 5,
            out_specs=(vmem, vmem),
            scratch_shapes=[
                pltpu.VMEM((n, n + 2 * width), f32),
            ],
            compiler_params=params,
            cost_estimate=pl.CostEstimate(flops=COST, bytes_accessed=0, transcendentals=0),
            name="leaf_solve",
        )(*local(owners, matrix, coupling, residual, inverse))

    if paced:
        steps = gather_steps(leaves)
        pair = [own]
        exchange(pair, "leaf", leaves, steps[0])
        inverse = invert()
        data = [
            pl.pallas_call(
                functools.partial(pack_kernel, leaves),
                out_shape=pltpu.VMEM((1, 3 * groups * band + groups, width), f32),
                in_specs=[vmem, vmem],
                out_specs=vmem,
                compiler_params=params,
                name="node_pack",
            )(*local(*pair))
        ]
        hold(data, inverse)
        exchange(data, "leaf", leaves, steps[1])
        solved, message = solve(*near, inverse)
        messages = [message]
        exchange(messages, "leaf", leaves, steps[-2])
        for step in steps[2:-1]:
            hold(data, messages[-1])
            exchange(data, "leaf", leaves, step)
        for step in steps[:-2]:
            exchange(messages, "leaf", leaves, step)
        hold(data, messages[-1])
        for pieces in (messages, data):
            exchange(pieces, "leaf", leaves, steps[-1])
        node_blocks = pl.pallas_call(
            functools.partial(assemble_kernel, leaves, source_offsets(steps[1:]), groups, band),
            out_shape=(
                pltpu.VMEM((groups, width // 2 + 8, width), f32),
                pltpu.VMEM((groups, width, size), f32),
            ),
            in_specs=[vmem] * len(data),
            out_specs=(vmem, vmem),
            compiler_params=params,
            name="node_assemble",
        )(*local(*data))
    else:
        rank = lax.axis_index("leaf")
        placed = lax.dynamic_update_slice(
            jnp.zeros((groups, width), f32), node_rhs, (jnp.zeros((), jnp.int32), rank * band)
        )
        every = lax.all_gather(
            jnp.concatenate([node_matrix, node_link], axis=0), "leaf", axis=1, tiled=True
        )
        blocks = every[:groups]
        half = width // 2
        row, col = grid_of(half, width)
        tops = jnp.where(col < row, jnp.roll(blocks[:, half:], half, 2), blocks[:, :half])
        shift = lax.psum(placed, "leaf")
        diagonal = jnp.where(
            jnp.arange(width) < half, 0.0, jnp.diagonal(blocks, axis1=1, axis2=2)
        )
        tails = jnp.stack([-shift, diagonal] + [jnp.zeros_like(shift)] * 6, axis=1)
        node_blocks = [jnp.concatenate([tops, tails], axis=1), every[groups:]]
        inverse = invert()
        solved, message = solve(*near, inverse)
        if doubling:
            messages = doubled(message, "leaf", leaves)
        else:
            messages = [lax.all_gather(message, "leaf", axis=0, tiled=True)]

    early = messages[:-1] or messages
    partial = pl.pallas_call(
        sum_kernel,
        out_shape=pltpu.VMEM((groups, width // 2 + 8, width), f32),
        in_specs=[vmem] * len(early),
        out_specs=vmem,
        compiler_params=params,
        cost_estimate=pl.CostEstimate(flops=COST // 4, bytes_accessed=0, transcendentals=0),
        name="node_sum",
    )(*local(*early))
    late = messages[len(early) :]

    answers, part = pl.pallas_call(
        node_kernel,
        out_shape=(
            pltpu.VMEM((groups, size + 16, width), f32),
            pltpu.VMEM((size // 2 + 8, size), f32),
        ),
        in_specs=[vmem] * (3 + len(late)),
        out_specs=(vmem, vmem),
        scratch_shapes=[
            pltpu.VMEM((groups, width, width), f32),
            pltpu.VMEM((groups, size + 16, width), f32),
            pltpu.VMEM((width, width + 2 * size), f32),
        ],
        compiler_params=params,
        name="node_solve",
    )(*local(*node_blocks, partial, *late))

    others = other_parts(part, "grp", sets)
    prepared = pl.pallas_call(
        functools.partial(prepare_kernel, sets),
        out_shape=(
            pltpu.VMEM((size, size), f32),
            pltpu.VMEM((16, size), f32),
            pltpu.VMEM((size, size), bf16),
            pltpu.VMEM((groups, size, width), f32),
            pltpu.VMEM((groups, width), f32),
            pltpu.VMEM((slots, size, n), f32),
            pltpu.VMEM((slots, 8, n), f32),
        ),
        in_specs=[vmem] * 6,
        out_specs=[vmem] * 7,
        compiler_params=params,
        cost_estimate=pl.CostEstimate(flops=COST // 2, bytes_accessed=0, transcendentals=0),
        name="root_prepare",
    )(*local(owners, part, root_matrix, root_row, answers, solved))

    leaf_dir, node_dir, root_dir = pl.pallas_call(
        functools.partial(root_kernel, sets, band),
        out_shape=(
            jax.ShapeDtypeStruct((slots, n), f32),
            jax.ShapeDtypeStruct((groups, band), f32),
            jax.ShapeDtypeStruct((1, size), f32),
        ),
        in_specs=[vmem] * (7 + len(others)),
        out_specs=(vmem, vmem, vmem),
        scratch_shapes=[
            pltpu.VMEM((size, size), f32),
            pltpu.VMEM((16, size), f32),
            pltpu.VMEM((size, 2 * size), f32),
        ],
        compiler_params=params,
        name="root_solve",
    )(*local(*prepared, *others))
    return leaf_dir, node_dir, root_dir[0]


def solution(mesh):
    return jax.shard_map(
        functools.partial(body, mesh.shape["leaf"], mesh.shape["grp"]),
        mesh=mesh,
        in_specs=(
            P(("leaf", "grp")),
            P(("leaf", "grp"), None, None),
            P(("leaf", "grp"), None, None),
            P(("leaf", "grp"), None),
            P("grp", "leaf", None),
            P("grp", "leaf", None),
            P("grp", "leaf"),
            P(),
            P(),
        ),
        out_specs=(P(("leaf", "grp"), None), P("grp", "leaf"), P()),
        check_vma=False,
    )
```

```python
import functools

import jax
import jax.numpy as jnp
from jax import lax
from jax.experimental import pallas as pl
from jax.experimental.pallas import tpu as pltpu
from jax.sharding import PartitionSpec as P

f32 = jnp.float32
bf16 = jnp.bfloat16
FLOOR = 0.1
STEPS = 5
ROOT_STEPS = 6
WARM_STEPS = 3
COST = 3_000_000_000
KERNEL_VMEM = 24 << 20
ACCEPT = 4e-5


def mul(a, b):
    return jnp.dot(a, b, preferred_element_type=f32)


def split(a):
    high = a.astype(bf16)
    return high, (a - high.astype(f32)).astype(bf16)


def split3(a):
    high = a.astype(bf16)
    rest = a - high.astype(f32)
    mid = rest.astype(bf16)
    return high, mid, (rest - mid.astype(f32)).astype(bf16)


def beside(*parts):
    return jnp.concatenate(parts, axis=1)


def above(*parts):
    return jnp.concatenate(parts, axis=0)


def mul3(a, b):
    ah, al = split(a)
    bh, bl = split(b)
    return mul(beside(ah, ah, al), above(bh, bl, bh))


def grid_of(rows, cols):
    return (
        lax.broadcasted_iota(jnp.int32, (rows, cols), 0),
        lax.broadcasted_iota(jnp.int32, (rows, cols), 1),
    )


def identity(n):
    row, col = grid_of(n, n)
    return (row == col).astype(f32)


def pack_symmetric(full, extra):
    n = full.shape[0]
    half = n // 2
    row, col = grid_of(half, n)
    lower = full[half:]
    moved = pltpu.roll(lower, half, 1)
    top = jnp.where(col < row, moved, full[:half])
    diagonal = jnp.sum(jnp.where(col == row + half, lower, 0.0), axis=0, keepdims=True)
    row8, _ = grid_of(8, n)
    tail = jnp.where(row8 == 0, jnp.broadcast_to(extra, (8, n)), 0.0)
    tail = jnp.where(row8 == 1, jnp.broadcast_to(diagonal, (8, n)), tail)
    return top, tail


def unpack_symmetric(top, diagonal):
    half, n = top.shape
    row, col = grid_of(half, n)
    flipped = jnp.concatenate([top, jnp.zeros_like(top)], axis=0).T
    upper = jnp.where((col < half) & (col < row), flipped[:half], top)
    inner = pltpu.roll(jnp.where(col < row, top, flipped[:half]), half, 1)
    inner = jnp.where(col == row + half, jnp.broadcast_to(diagonal, (half, n)), inner)
    lower = jnp.where(col < half, flipped[half:], inner)
    return jnp.concatenate([upper, lower], axis=0)


def coarse_inverse(bound, matrices, steps):
    one = identity(matrices[0].shape[0])
    alpha = 2.0 / (bound + FLOOR)
    delta = (bound - FLOOR) / (bound + FLOOR)
    square = delta * delta
    scale = 2.0 / (2.0 - square)
    scaled = [alpha * m for m in matrices]
    errors = [(one - s).astype(bf16) for s in scaled]
    inverses = [((scale * alpha) * (2.0 * one - s)).astype(bf16) for s in scaled]
    for _ in range(steps - 1):
        errors = [(scale * (mul(e, e) - (0.5 * square) * one)).astype(bf16) for e in errors]
        delta = square / (2.0 - square)
        square = delta * delta
        scale = 2.0 / (2.0 - square)
        inverses = [
            (scale * (v.astype(f32) + mul(e, v))).astype(bf16) for e, v in zip(errors, inverses)
        ]
    return inverses


def warm_inverse(matrix, near, low, steps):
    one = identity(matrix.shape[0])
    product = mul(near, matrix.astype(bf16))
    bound = jnp.maximum(norm_bound(product), 2.0 * low)
    alpha = 2.0 / (bound + low)
    delta = (bound - low) / (bound + low)
    square = delta * delta
    scale = 2.0 / (2.0 - square)
    error = (one - alpha * product).astype(bf16)
    inverse = (alpha * near.astype(f32)).astype(bf16)
    for step in range(steps):
        inverse = (scale * (inverse.astype(f32) + mul(error, inverse))).astype(bf16)
        if step + 1 < steps:
            error = (scale * (mul(error, error) - (0.5 * square) * one)).astype(bf16)
            delta = square / (2.0 - square)
            square = delta * delta
            scale = 2.0 / (2.0 - square)
    return inverse


def finish(matrices, inverses, rights):
    errors = [
        identity(m.shape[0]) - mul(beside(v, v), above(*split(m)))
        for m, v in zip(matrices, inverses)
    ]
    pieces = [split(e) for e in errors]
    squares = [mul(h, h).astype(bf16) for h, _ in pieces]
    first = []
    for right, (eh, el) in zip(rights, pieces):
        rh, rl = split(right)
        first.append(right + mul(beside(rh, rh, rl), above(eh, el, eh)))
    second = [mul(z.astype(bf16), s) for z, s in zip(first, squares)]
    found = [
        mul(beside(*split(z + d)), above(v, v)) for z, d, v in zip(first, second, inverses)
    ]
    return found, [misfits(d, z) for z, d in zip(first, second)]


def misfits(change, values):
    got = jnp.sum(change * change, axis=1, keepdims=True)
    allowed = ACCEPT * jnp.sum(values * values, axis=1, keepdims=True)
    return jnp.where(got <= allowed, 0.0, 1.0)


def eliminate(work):
    n, width = work.shape

    def step(k, carry):
        row, col = grid_of(8, width)
        base = pl.multiple_of((k // 8) * 8, 8)
        block = work[pl.ds(base, 8), :]
        pivot_row = jnp.sum(jnp.where(row == k - base, block, 0.0), axis=0, keepdims=True)
        pivot = jnp.sum(jnp.where(col[:1] == k, pivot_row, 0.0), axis=1, keepdims=True)
        scaled = pivot_row / pivot
        full = work[...]
        row, col = grid_of(n, width)
        column = jnp.sum(jnp.where(col == k, full, 0.0), axis=1, keepdims=True)
        work[...] = jnp.where(row == k, scaled, full - column * scaled)
        return carry

    lax.fori_loop(0, n, step, 0)


def solve_again(work, matrix, right):
    n, rows = matrix.shape[0], right.shape[0]
    work[:, :n] = matrix
    padded = above(right, jnp.zeros((work.shape[1] - n - rows, n), f32))
    work[:, n:] = padded.T
    eliminate(work)
    return work[:, n:].T[:rows]


def norm_bound(*matrices):
    sums = [jnp.sum(jnp.abs(m), axis=0, keepdims=True) for m in matrices]
    most = sums[0]
    for other in sums[1:]:
        most = jnp.maximum(most, other)
    return jnp.max(most, axis=1, keepdims=True)


def stage_kernel(parent, matrix, link, rhs, *refs):
    matrix_rows, link_rows, rhs_rows, sems = refs[-4:]
    count = (len(refs) - 6) // 2
    rest, owners, own, targets = refs[:count], refs[count], refs[count + 1], refs[count + 2 : -4]
    pairs = ((matrix, matrix_rows), (link, link_rows), (rhs, rhs_rows), *zip(rest, targets))
    copies = [
        pltpu.make_async_copy(source, target, sems.at[i])
        for i, (source, target) in enumerate(pairs)
    ]
    for copy in copies:
        copy.start()
    for s in range(owners.shape[0]):
        owners[s] = jnp.full(owners.shape[1:], parent[s].astype(f32))
    groups, band, _ = matrix_rows.shape
    rows = groups * band
    own[0, 2 * rows :, :] = jnp.zeros((groups, own.shape[2]), f32)
    for copy in copies[:3]:
        copy.wait()
    for q in range(groups):
        own[0, q * band : (q + 1) * band, :] = matrix_rows[q]
        own[0, rows + q * band : rows + (q + 1) * band, :] = link_rows[q]
    own[0, 2 * rows :, :band] = rhs_rows[...]
    for copy in copies[3:]:
        copy.wait()


def invert_kernel(matrix, inverse):
    for s in range(matrix.shape[0]):
        block = matrix[s]
        inverse[s] = coarse_inverse(norm_bound(block), [block], STEPS)[0]


def leaf_kernel(owners, matrix, coupling, residual, inverse, solved, message, work):
    n = matrix.shape[1]
    width = coupling.shape[2]
    for s in range(matrix.shape[0]):

        def right_side():
            return above(coupling[s].T, jnp.broadcast_to(residual[s : s + 1, :], (16, n)))

        def give(found):
            solved[s] = found
            product = mul3(found, coupling[s])
            top, tail = pack_symmetric(product[:width], product[width : width + 1])
            row8, _ = grid_of(8, width)
            message[s, : width // 2, :] = top
            message[s, width // 2 :, :] = jnp.where(row8 == 2, owners[s], tail)

        found, bad = finish([matrix[s]], [inverse[s]], [right_side()])
        give(found[0])

        @pl.when(jnp.sum(bad[0]) > 0.0)
        def _():
            give(solve_again(work, matrix[s], right_side()))


def pack_kernel(leaves, own, other, packed):
    n = own.shape[2]
    half = n // 2
    band = half // (leaves // 2)
    groups = own.shape[1] // (2 * band + 1)
    rows = groups * band
    here = lax.axis_index("leaf")
    is_top = here < leaves // 2
    place = lax.rem(here, leaves // 2) * band
    top = jnp.where(is_top, own[0], other[0])
    low = jnp.where(is_top, other[0], own[0])
    row, col = grid_of(band, n)
    row = row + place
    diagonals = []
    for q in range(groups):
        at = slice(q * band, (q + 1) * band)
        packed[0, at, :] = jnp.where(col < row, pltpu.roll(low[at], half, 1), top[at])
        diagonals.append(
            jnp.sum(jnp.where(col == row + half, low[at], 0.0), axis=0, keepdims=True)
        )
    packed[0, rows : 2 * rows, :] = top[rows : 2 * rows]
    packed[0, 2 * rows : 3 * rows, :] = low[rows : 2 * rows]
    _, col = grid_of(groups, n)
    diagonal = pltpu.roll(above(*diagonals), lax.rem(half + 2 * band - place, n), 1)
    last = jnp.where(col < 2 * band, pltpu.roll(low[2 * rows :], band, 1), diagonal)
    last = jnp.where(col < band, top[2 * rows :], last)
    packed[0, 3 * rows :, :] = jnp.where(col < 3 * band, last, 0.0)


def assemble_kernel(leaves, sources, groups, band, *refs):
    data = refs[:-2]
    regular, links = refs[-2:]
    n = regular.shape[2]
    half = n // 2
    rows = groups * band
    here = lax.axis_index("leaf")
    row, col = grid_of(groups, n)
    at = 0
    shift = jnp.zeros((groups, n), f32)
    diagonal = jnp.zeros((groups, n), f32)
    for piece in data:
        for j in range(piece.shape[0]):
            place = lax.rem(here ^ sources[at], leaves // 2) * band
            place = pl.multiple_of(place, band)
            at += 1
            for q in range(groups):
                regular[q, pl.ds(place, band), :] = piece[j, q * band : (q + 1) * band, :]
                start = rows + q * band
                links[q, pl.ds(place, band), :] = piece[j, start : start + band, :]
                start = start + rows
                links[q, pl.ds(half + place, band), :] = piece[j, start : start + band, :]
            last = piece[j, 3 * rows :, :]
            first = jnp.where(col < band, last, 0.0)
            second = jnp.where((col >= band) & (col < 2 * band), last, 0.0)
            third = jnp.where(col >= 2 * band, last, 0.0)
            shift = shift + pltpu.roll(first, place, 1)
            shift = shift + pltpu.roll(second, lax.rem(half + place - band + n, n), 1)
            diagonal = diagonal + pltpu.roll(third, lax.rem(half + place - 2 * band + n, n), 1)
    row8, _ = grid_of(8, n)
    for q in range(groups):
        tail = jnp.where(row8 == 0, -shift[q : q + 1], 0.0)
        regular[q, half:, :] = jnp.where(row8 == 1, diagonal[q : q + 1], tail)


def add_messages(sums, messages):
    if not messages:
        return sums
    row = messages[0].shape[1] - 6
    for piece in messages:
        for j in range(piece.shape[0]):
            message = piece[j]
            owner = message[row : row + 1, :]
            sums = [x + jnp.where(owner == q, message, 0.0) for q, x in enumerate(sums)]
    return sums


def sum_kernel(*refs):
    sums = refs[-1]
    groups = sums.shape[0]
    zero = jnp.zeros(sums.shape[1:], f32)
    for q, total in enumerate(add_messages([zero] * groups, refs[:-1])):
        sums[q] = total


def node_kernel(regular, links, partial, *refs):
    messages = refs[:-5]
    answers, message, full, rights, work = refs[-5:]
    groups, n, width = links.shape
    half = n // 2
    sums = add_messages([regular[q] + partial[q] for q in range(groups)], messages)
    tops = [x[:half] for x in sums]
    tails = [x[half:] for x in sums]
    for q in range(groups):
        full[q] = unpack_symmetric(tops[q], tails[q][1:2])
        rights[q, :width] = links[q].T
        rights[q, width:] = jnp.broadcast_to(tails[q][:1], (16, n))
    blocks = [full[q] for q in range(groups)]
    inverses = coarse_inverse(norm_bound(*blocks), blocks, STEPS)
    found, bad = finish(blocks, inverses, [rights[q] for q in range(groups)])

    def give(found):
        total = None
        for q in range(groups):
            answers[q] = found(q)
            part = mul3(found(q), links[q])
            total = part if q == 0 else total + part
        top, tail = pack_symmetric(total[:width], total[width : width + 1])
        message[: width // 2, :] = top
        message[width // 2 :, :] = tail

    give(lambda q: found[q])

    @pl.when(jnp.sum(sum(bad)) > 0.0)
    def _():
        for q in range(groups):
            answers[q] = solve_again(work, full[q], rights[q])
        give(lambda q: answers[q])


def prepare_kernel(
    sets, owners, part, matrix, rhs, answers, solved, base, base_row, near, moves, fixed, leaf_moves, leaf_fixed
):
    size = matrix.shape[0]
    half = size // 2
    groups, _, n = answers.shape
    mine = unpack_symmetric(part[:half, :], part[half + 1 : half + 2, :])
    base[...] = matrix[...] + mine
    guess = matrix[...] + sets * mine
    near[...] = coarse_inverse(norm_bound(guess), [guess], ROOT_STEPS)[0]
    base_row[...] = jnp.broadcast_to(rhs[...] - part[half : half + 1, :], base_row.shape)
    for q in range(groups):
        fixed[q : q + 1, :] = answers[q, size : size + 1, :]
        moves[q] = answers[q, :size, :]
    for s in range(solved.shape[0]):
        owner = owners[s, :1, :1]
        own = jnp.zeros_like(answers[0])
        for q in range(groups):
            own = jnp.where(owner == q, answers[q], own)
        product = mul3(own, solved[s, :n, :])
        live = owner >= 0.0
        leaf_moves[s] = jnp.where(live, -product[:size], 0.0)
        last = solved[s, n : n + 8, :] - product[size : size + 8]
        leaf_fixed[s] = jnp.where(live, last, 0.0)


def root_kernel(
    sets, band, base, base_row, near, moves, fixed, leaf_moves, leaf_fixed, *refs
):
    others = refs[:-5]
    leaf_dir, node_dir, root_dir, full, work = refs[-5:]
    size = base.shape[0]
    half = size // 2
    groups, _, n = moves.shape
    system = base[...]
    right = base_row[...]
    for other in others:
        system = system + unpack_symmetric(other[:half, :], other[half + 1 : half + 2, :])
        right = right - other[half : half + 1, :]
    full[...] = system
    inverse = warm_inverse(system, near[...], 1.0 / sets, WARM_STEPS)
    found, bad = finish([system], [inverse], [right])

    def give(answer):
        root_dir[...] = answer
        column = jnp.broadcast_to(answer, (size, size)).T
        each = [jnp.sum(column * moves[q], axis=0, keepdims=True) for q in range(groups)]
        every = above(*each) + fixed[...]
        if band == n:
            node_dir[...] = every
        else:
            me = lax.axis_index("leaf")
            node_dir[...] = pltpu.roll(every, lax.rem(n - me * band, n), 1)[:, :band]
        wide = leaf_moves.shape[2] // size
        for s in range(leaf_moves.shape[0]):
            terms = beside(*[column] * wide) * leaf_moves[s]
            leaf_dir[s : s + 1, :] = jnp.sum(terms, axis=0, keepdims=True) + leaf_fixed[s, :1, :]

    give(found[0][:1])

    @pl.when(jnp.sum(bad[0]) > 0.0)
    def _():
        give(solve_again(work, full[...], right)[:1])


def gather_steps(extent):
    steps = []
    while extent > 1:
        extent //= 2
        steps.append(extent)
    return steps


def moved(values, axis, extent, distance):
    return lax.ppermute(values, axis, [(i, i ^ distance) for i in range(extent)])


def exchange(pieces, axis, extent, distance):
    sent = pieces[0] if len(pieces) == 1 else jnp.concatenate(pieces, axis=0)
    pieces.append(moved(sent, axis, extent, distance))


def doubled(values, axis, extent):
    pieces = [values]
    for distance in gather_steps(extent):
        exchange(pieces, axis, extent, distance)
    return pieces


def hold(pieces, value):
    pieces[-1] = lax.optimization_barrier((value, pieces[-1]))[1]


def source_offsets(steps):
    offsets = [0]
    for distance in steps:
        offsets = offsets + [o ^ distance for o in offsets]
    return tuple(offsets)


def other_parts(values, axis, extent):
    if extent == 1:
        return []
    if extent & (extent - 1):
        return [lax.psum(values, axis) - values]
    steps = gather_steps(extent)
    pieces = []
    for distance in reversed(steps):
        pieces.append(moved(values, axis, extent, distance))
        values = values + pieces[-1]
    return pieces


def remote(*values):
    return [pltpu.with_memory_space_constraint(v, pltpu.HBM) for v in values]


def local(*values):
    return [pltpu.with_memory_space_constraint(v, pltpu.VMEM) for v in values]


def body(
    leaves,
    sets,
    slot_parent,
    leaf_matrix,
    coupling,
    leaf_residual_rows,
    node_matrix,
    node_link,
    node_rhs,
    root_matrix,
    root_rhs,
):
    slots, n = leaf_residual_rows.shape
    groups, band, width = node_matrix.shape
    size = node_link.shape[2]
    doubling = leaves & (leaves - 1) == 0
    vmem = pl.BlockSpec(memory_space=pltpu.VMEM)
    smem = pl.BlockSpec(memory_space=pltpu.SMEM)
    params = pltpu.CompilerParams(vmem_limit_bytes=KERNEL_VMEM)

    paced = doubling and band % 8 == 0 and 4 <= leaves and 3 * band <= width
    hbm = pl.BlockSpec(memory_space=pltpu.HBM)
    nodes = [node_matrix, node_link, node_rhs]
    staged = [leaf_matrix, coupling, leaf_residual_rows, root_matrix, root_rhs[None, :]]
    owners, own, *near, root_matrix, root_row = pl.pallas_call(
        stage_kernel,
        out_shape=(
            pltpu.VMEM((slots, 8, width), f32),
            pltpu.VMEM((1, 2 * groups * band + groups, width), f32),
            *[pltpu.VMEM(a.shape, f32) for a in staged],
        ),
        in_specs=[smem] + [hbm] * (3 + len(staged)),
        out_specs=[vmem] * (2 + len(staged)),
        scratch_shapes=[pltpu.VMEM(a.shape, f32) for a in nodes]
        + [pltpu.SemaphoreType.DMA((3 + len(staged),))],
        compiler_params=params,
        name="stage",
    )(slot_parent, *remote(*nodes, *staged))
    def invert():
        return pl.pallas_call(
            invert_kernel,
            out_shape=pltpu.VMEM((slots, n, n), bf16),
            in_specs=[vmem],
            out_specs=vmem,
            compiler_params=params,
            cost_estimate=pl.CostEstimate(flops=COST, bytes_accessed=0, transcendentals=0),
            name="leaf_invert",
        )(*local(near[0]))

    def solve(matrix, coupling, residual, inverse):
        return pl.pallas_call(
            leaf_kernel,
            out_shape=(
                pltpu.VMEM((slots, width + 16, n), f32),
                pltpu.VMEM((slots, width // 2 + 8, width), f32),
            ),
            in_specs=[vmem] * 5,
            out_specs=(vmem, vmem),
            scratch_shapes=[
                pltpu.VMEM((n, n + 2 * width), f32),
            ],
            compiler_params=params,
            cost_estimate=pl.CostEstimate(flops=COST, bytes_accessed=0, transcendentals=0),
            name="leaf_solve",
        )(*local(owners, matrix, coupling, residual, inverse))

    if paced:
        steps = gather_steps(leaves)
        pair = [own]
        exchange(pair, "leaf", leaves, steps[0])
        inverse = invert()
        data = [
            pl.pallas_call(
                functools.partial(pack_kernel, leaves),
                out_shape=pltpu.VMEM((1, 3 * groups * band + groups, width), f32),
                in_specs=[vmem, vmem],
                out_specs=vmem,
                compiler_params=params,
                name="node_pack",
            )(*local(*pair))
        ]
        hold(data, inverse)
        exchange(data, "leaf", leaves, steps[1])
        solved, message = solve(*near, inverse)
        messages = [message]
        exchange(messages, "leaf", leaves, steps[-2])
        for step in steps[2:-1]:
            hold(data, messages[-1])
            exchange(data, "leaf", leaves, step)
        for step in steps[:-2]:
            exchange(messages, "leaf", leaves, step)
        hold(data, messages[-1])
        for pieces in (messages, data):
            exchange(pieces, "leaf", leaves, steps[-1])
        node_blocks = pl.pallas_call(
            functools.partial(assemble_kernel, leaves, source_offsets(steps[1:]), groups, band),
            out_shape=(
                pltpu.VMEM((groups, width // 2 + 8, width), f32),
                pltpu.VMEM((groups, width, size), f32),
            ),
            in_specs=[vmem] * len(data),
            out_specs=(vmem, vmem),
            compiler_params=params,
            name="node_assemble",
        )(*local(*data))
    else:
        rank = lax.axis_index("leaf")
        placed = lax.dynamic_update_slice(
            jnp.zeros((groups, width), f32), node_rhs, (jnp.zeros((), jnp.int32), rank * band)
        )
        every = lax.all_gather(
            jnp.concatenate([node_matrix, node_link], axis=0), "leaf", axis=1, tiled=True
        )
        blocks = every[:groups]
        half = width // 2
        row, col = grid_of(half, width)
        tops = jnp.where(col < row, jnp.roll(blocks[:, half:], half, 2), blocks[:, :half])
        shift = lax.psum(placed, "leaf")
        diagonal = jnp.where(
            jnp.arange(width) < half, 0.0, jnp.diagonal(blocks, axis1=1, axis2=2)
        )
        tails = jnp.stack([-shift, diagonal] + [jnp.zeros_like(shift)] * 6, axis=1)
        node_blocks = [jnp.concatenate([tops, tails], axis=1), every[groups:]]
        inverse = invert()
        solved, message = solve(*near, inverse)
        if doubling:
            messages = doubled(message, "leaf", leaves)
        else:
            messages = [lax.all_gather(message, "leaf", axis=0, tiled=True)]

    early = messages[:-1] or messages
    partial = pl.pallas_call(
        sum_kernel,
        out_shape=pltpu.VMEM((groups, width // 2 + 8, width), f32),
        in_specs=[vmem] * len(early),
        out_specs=vmem,
        compiler_params=params,
        cost_estimate=pl.CostEstimate(flops=COST // 4, bytes_accessed=0, transcendentals=0),
        name="node_sum",
    )(*local(*early))
    late = messages[len(early) :]

    answers, part = pl.pallas_call(
        node_kernel,
        out_shape=(
            pltpu.VMEM((groups, size + 16, width), f32),
            pltpu.VMEM((size // 2 + 8, size), f32),
        ),
        in_specs=[vmem] * (3 + len(late)),
        out_specs=(vmem, vmem),
        scratch_shapes=[
            pltpu.VMEM((groups, width, width), f32),
            pltpu.VMEM((groups, size + 16, width), f32),
            pltpu.VMEM((width, width + 2 * size), f32),
        ],
        compiler_params=params,
        name="node_solve",
    )(*local(*node_blocks, partial, *late))

    others = other_parts(part, "grp", sets)
    prepared = pl.pallas_call(
        functools.partial(prepare_kernel, sets),
        out_shape=(
            pltpu.VMEM((size, size), f32),
            pltpu.VMEM((16, size), f32),
            pltpu.VMEM((size, size), bf16),
            pltpu.VMEM((groups, size, width), f32),
            pltpu.VMEM((groups, width), f32),
            pltpu.VMEM((slots, size, n), f32),
            pltpu.VMEM((slots, 8, n), f32),
        ),
        in_specs=[vmem] * 6,
        out_specs=[vmem] * 7,
        compiler_params=params,
        cost_estimate=pl.CostEstimate(flops=COST // 2, bytes_accessed=0, transcendentals=0),
        name="root_prepare",
    )(*local(owners, part, root_matrix, root_row, answers, solved))

    leaf_dir, node_dir, root_dir = pl.pallas_call(
        functools.partial(root_kernel, sets, band),
        out_shape=(
            jax.ShapeDtypeStruct((slots, n), f32),
            jax.ShapeDtypeStruct((groups, band), f32),
            jax.ShapeDtypeStruct((1, size), f32),
        ),
        in_specs=[vmem] * (7 + len(others)),
        out_specs=(vmem, vmem, vmem),
        scratch_shapes=[
            pltpu.VMEM((size, size), f32),
            pltpu.VMEM((size, 2 * size), f32),
        ],
        compiler_params=params,
        name="root_solve",
    )(*local(*prepared, *others))
    return leaf_dir, node_dir, root_dir[0]


def solution(mesh):
    return jax.shard_map(
        functools.partial(body, mesh.shape["leaf"], mesh.shape["grp"]),
        mesh=mesh,
        in_specs=(
            P(("leaf", "grp")),
            P(("leaf", "grp"), None, None),
            P(("leaf", "grp"), None, None),
            P(("leaf", "grp"), None),
            P("grp", "leaf", None),
            P("grp", "leaf", None),
            P("grp", "leaf"),
            P(),
            P(),
        ),
        out_specs=(P(("leaf", "grp"), None), P("grp", "leaf"), P()),
        check_vma=False,
    )
```

```python
import functools

import jax
import jax.numpy as jnp
from jax import lax
from jax.experimental import pallas as pl
from jax.experimental.pallas import tpu as pltpu
from jax.sharding import PartitionSpec as P

f32 = jnp.float32
bf16 = jnp.bfloat16
FLOOR = 0.1
STEPS = 5
ROOT_STEPS = 6
WARM_STEPS = 3
COST = 3_000_000_000
KERNEL_VMEM = 24 << 20
ACCEPT = 4e-5


def mul(a, b):
    return jnp.dot(a, b, preferred_element_type=f32)


def split(a):
    high = a.astype(bf16)
    return high, (a - high.astype(f32)).astype(bf16)


def split3(a):
    high = a.astype(bf16)
    rest = a - high.astype(f32)
    mid = rest.astype(bf16)
    return high, mid, (rest - mid.astype(f32)).astype(bf16)


def beside(*parts):
    return jnp.concatenate(parts, axis=1)


def above(*parts):
    return jnp.concatenate(parts, axis=0)


def mul3(a, b):
    ah, al = split(a)
    bh, bl = split(b)
    return mul(beside(ah, ah, al), above(bh, bl, bh))


def grid_of(rows, cols):
    return (
        lax.broadcasted_iota(jnp.int32, (rows, cols), 0),
        lax.broadcasted_iota(jnp.int32, (rows, cols), 1),
    )


def identity(n):
    row, col = grid_of(n, n)
    return (row == col).astype(f32)


def pack_symmetric(full, extra):
    n = full.shape[0]
    half = n // 2
    row, col = grid_of(half, n)
    lower = full[half:]
    moved = pltpu.roll(lower, half, 1)
    top = jnp.where(col < row, moved, full[:half])
    diagonal = jnp.sum(jnp.where(col == row + half, lower, 0.0), axis=0, keepdims=True)
    row8, _ = grid_of(8, n)
    tail = jnp.where(row8 == 0, jnp.broadcast_to(extra, (8, n)), 0.0)
    tail = jnp.where(row8 == 1, jnp.broadcast_to(diagonal, (8, n)), tail)
    return top, tail


def unpack_symmetric(top, diagonal):
    half, n = top.shape
    row, col = grid_of(half, n)
    flipped = jnp.concatenate([top, jnp.zeros_like(top)], axis=0).T
    upper = jnp.where((col < half) & (col < row), flipped[:half], top)
    inner = pltpu.roll(jnp.where(col < row, top, flipped[:half]), half, 1)
    inner = jnp.where(col == row + half, jnp.broadcast_to(diagonal, (half, n)), inner)
    lower = jnp.where(col < half, flipped[half:], inner)
    return jnp.concatenate([upper, lower], axis=0)


def coarse_inverse(bound, matrices, steps):
    one = identity(matrices[0].shape[0])
    alpha = 2.0 / (bound + FLOOR)
    delta = (bound - FLOOR) / (bound + FLOOR)
    square = delta * delta
    scale = 2.0 / (2.0 - square)
    scaled = [alpha * m for m in matrices]
    errors = [(one - s).astype(bf16) for s in scaled]
    inverses = [((scale * alpha) * (2.0 * one - s)).astype(bf16) for s in scaled]
    for _ in range(steps - 1):
        errors = [(scale * (mul(e, e) - (0.5 * square) * one)).astype(bf16) for e in errors]
        delta = square / (2.0 - square)
        square = delta * delta
        scale = 2.0 / (2.0 - square)
        inverses = [
            (scale * (v.astype(f32) + mul(e, v))).astype(bf16) for e, v in zip(errors, inverses)
        ]
    return inverses


def warm_inverse(matrix, near, low, steps):
    one = identity(matrix.shape[0])
    product = mul(near, matrix.astype(bf16))
    bound = jnp.maximum(norm_bound(product), 2.0 * low)
    alpha = 2.0 / (bound + low)
    delta = (bound - low) / (bound + low)
    square = delta * delta
    scale = 2.0 / (2.0 - square)
    error = (one - alpha * product).astype(bf16)
    inverse = (alpha * near.astype(f32)).astype(bf16)
    for step in range(steps):
        inverse = (scale * (inverse.astype(f32) + mul(error, inverse))).astype(bf16)
        if step + 1 < steps:
            error = (scale * (mul(error, error) - (0.5 * square) * one)).astype(bf16)
            delta = square / (2.0 - square)
            square = delta * delta
            scale = 2.0 / (2.0 - square)
    return inverse


def finish(matrices, inverses, rights):
    errors = [
        identity(m.shape[0]) - mul(beside(v, v), above(*split(m)))
        for m, v in zip(matrices, inverses)
    ]
    pieces = [split(e) for e in errors]
    squares = [mul(h, h).astype(bf16) for h, _ in pieces]
    first = []
    for right, (eh, el) in zip(rights, pieces):
        rh, rl = split(right)
        first.append(right + mul(beside(rh, rh, rl), above(eh, el, eh)))
    second = [mul(z.astype(bf16), s) for z, s in zip(first, squares)]
    found = [
        mul(beside(*split(z + d)), above(v, v)) for z, d, v in zip(first, second, inverses)
    ]
    return found, [misfits(d, z) for z, d in zip(first, second)]


def misfits(change, values):
    got = jnp.sum(change * change, axis=1, keepdims=True)
    allowed = ACCEPT * jnp.sum(values * values, axis=1, keepdims=True)
    return jnp.where(got <= allowed, 0.0, 1.0)


def eliminate(work):
    n, width = work.shape

    def step(k, carry):
        row, col = grid_of(8, width)
        base = pl.multiple_of((k // 8) * 8, 8)
        block = work[pl.ds(base, 8), :]
        pivot_row = jnp.sum(jnp.where(row == k - base, block, 0.0), axis=0, keepdims=True)
        pivot = jnp.sum(jnp.where(col[:1] == k, pivot_row, 0.0), axis=1, keepdims=True)
        scaled = pivot_row / pivot
        full = work[...]
        row, col = grid_of(n, width)
        column = jnp.sum(jnp.where(col == k, full, 0.0), axis=1, keepdims=True)
        work[...] = jnp.where(row == k, scaled, full - column * scaled)
        return carry

    lax.fori_loop(0, n, step, 0)


def solve_again(work, matrix, right):
    n, rows = matrix.shape[0], right.shape[0]
    work[:, :n] = matrix
    padded = above(right, jnp.zeros((work.shape[1] - n - rows, n), f32))
    work[:, n:] = padded.T
    eliminate(work)
    return work[:, n:].T[:rows]


def norm_bound(*matrices):
    sums = [jnp.sum(jnp.abs(m), axis=0, keepdims=True) for m in matrices]
    most = sums[0]
    for other in sums[1:]:
        most = jnp.maximum(most, other)
    return jnp.max(most, axis=1, keepdims=True)


def stage_kernel(parent, matrix, link, rhs, *refs):
    matrix_rows, link_rows, rhs_rows, sems = refs[-4:]
    count = (len(refs) - 6) // 2
    rest, owners, own, targets = refs[:count], refs[count], refs[count + 1], refs[count + 2 : -4]
    pairs = ((matrix, matrix_rows), (link, link_rows), (rhs, rhs_rows), *zip(rest, targets))
    copies = [
        pltpu.make_async_copy(source, target, sems.at[i])
        for i, (source, target) in enumerate(pairs)
    ]
    for copy in copies:
        copy.start()
    for s in range(owners.shape[0]):
        owners[s] = jnp.full(owners.shape[1:], parent[s].astype(f32))
    groups, band, _ = matrix_rows.shape
    rows = groups * band
    own[0, 2 * rows :, :] = jnp.zeros((groups, own.shape[2]), f32)
    for copy in copies[:3]:
        copy.wait()
    for q in range(groups):
        own[0, q * band : (q + 1) * band, :] = matrix_rows[q]
        own[0, rows + q * band : rows + (q + 1) * band, :] = link_rows[q]
    own[0, 2 * rows :, :band] = rhs_rows[...]
    for copy in copies[3:]:
        copy.wait()


def invert_kernel(matrix, inverse):
    for s in range(matrix.shape[0]):
        block = matrix[s]
        inverse[s] = coarse_inverse(norm_bound(block), [block], STEPS)[0]


def leaf_kernel(owners, matrix, coupling, residual, inverse, solved, message, work):
    n = matrix.shape[1]
    width = coupling.shape[2]
    for s in range(matrix.shape[0]):

        def right_side():
            return above(coupling[s].T, jnp.broadcast_to(residual[s : s + 1, :], (16, n)))

        def give(found):
            solved[s] = found
            product = mul3(found, coupling[s])
            top, tail = pack_symmetric(product[:width], product[width : width + 1])
            row8, _ = grid_of(8, width)
            message[s, : width // 2, :] = top
            message[s, width // 2 :, :] = jnp.where(row8 == 2, owners[s], tail)

        found, bad = finish([matrix[s]], [inverse[s]], [right_side()])
        give(found[0])

        @pl.when(jnp.sum(bad[0]) > 0.0)
        def _():
            give(solve_again(work, matrix[s], right_side()))


def pack_kernel(leaves, own, other, packed):
    n = own.shape[2]
    half = n // 2
    band = half // (leaves // 2)
    groups = own.shape[1] // (2 * band + 1)
    rows = groups * band
    here = lax.axis_index("leaf")
    is_top = here < leaves // 2
    place = lax.rem(here, leaves // 2) * band
    top = jnp.where(is_top, own[0], other[0])
    low = jnp.where(is_top, other[0], own[0])
    row, col = grid_of(band, n)
    row = row + place
    diagonals = []
    for q in range(groups):
        at = slice(q * band, (q + 1) * band)
        packed[0, at, :] = jnp.where(col < row, pltpu.roll(low[at], half, 1), top[at])
        diagonals.append(
            jnp.sum(jnp.where(col == row + half, low[at], 0.0), axis=0, keepdims=True)
        )
    packed[0, rows : 2 * rows, :] = top[rows : 2 * rows]
    packed[0, 2 * rows : 3 * rows, :] = low[rows : 2 * rows]
    _, col = grid_of(groups, n)
    diagonal = pltpu.roll(above(*diagonals), lax.rem(half + 2 * band - place, n), 1)
    last = jnp.where(col < 2 * band, pltpu.roll(low[2 * rows :], band, 1), diagonal)
    last = jnp.where(col < band, top[2 * rows :], last)
    packed[0, 3 * rows :, :] = jnp.where(col < 3 * band, last, 0.0)


def assemble_kernel(leaves, sources, groups, band, *refs):
    data = refs[:-2]
    regular, links = refs[-2:]
    n = regular.shape[2]
    half = n // 2
    rows = groups * band
    here = lax.axis_index("leaf")
    row, col = grid_of(groups, n)
    at = 0
    shift = jnp.zeros((groups, n), f32)
    diagonal = jnp.zeros((groups, n), f32)
    for piece in data:
        for j in range(piece.shape[0]):
            place = lax.rem(here ^ sources[at], leaves // 2) * band
            place = pl.multiple_of(place, band)
            at += 1
            for q in range(groups):
                regular[q, pl.ds(place, band), :] = piece[j, q * band : (q + 1) * band, :]
                start = rows + q * band
                links[q, pl.ds(place, band), :] = piece[j, start : start + band, :]
                start = start + rows
                links[q, pl.ds(half + place, band), :] = piece[j, start : start + band, :]
            last = piece[j, 3 * rows :, :]
            first = jnp.where(col < band, last, 0.0)
            second = jnp.where((col >= band) & (col < 2 * band), last, 0.0)
            third = jnp.where(col >= 2 * band, last, 0.0)
            shift = shift + pltpu.roll(first, place, 1)
            shift = shift + pltpu.roll(second, lax.rem(half + place - band + n, n), 1)
            diagonal = diagonal + pltpu.roll(third, lax.rem(half + place - 2 * band + n, n), 1)
    row8, _ = grid_of(8, n)
    for q in range(groups):
        tail = jnp.where(row8 == 0, -shift[q : q + 1], 0.0)
        regular[q, half:, :] = jnp.where(row8 == 1, diagonal[q : q + 1], tail)


def add_messages(sums, messages):
    if not messages:
        return sums
    row = messages[0].shape[1] - 6
    for piece in messages:
        for j in range(piece.shape[0]):
            message = piece[j]
            owner = message[row : row + 1, :]
            sums = [x + jnp.where(owner == q, message, 0.0) for q, x in enumerate(sums)]
    return sums


def sum_kernel(*refs):
    sums = refs[-1]
    groups = sums.shape[0]
    zero = jnp.zeros(sums.shape[1:], f32)
    for q, total in enumerate(add_messages([zero] * groups, refs[:-1])):
        sums[q] = total


def node_kernel(regular, links, partial, *refs):
    messages = refs[:-5]
    answers, message, full, rights, work = refs[-5:]
    groups, n, width = links.shape
    half = n // 2
    sums = add_messages([regular[q] + partial[q] for q in range(groups)], messages)
    tops = [x[:half] for x in sums]
    tails = [x[half:] for x in sums]
    for q in range(groups):
        full[q] = unpack_symmetric(tops[q], tails[q][1:2])
        rights[q, :width] = links[q].T
        rights[q, width:] = jnp.broadcast_to(tails[q][:1], (16, n))
    blocks = [full[q] for q in range(groups)]
    inverses = coarse_inverse(norm_bound(*blocks), blocks, STEPS)
    found, bad = finish(blocks, inverses, [rights[q] for q in range(groups)])

    def give(found):
        total = None
        for q in range(groups):
            answers[q] = found(q)
            part = mul3(found(q), links[q])
            total = part if q == 0 else total + part
        top, tail = pack_symmetric(total[:width], total[width : width + 1])
        message[: width // 2, :] = top
        message[width // 2 :, :] = tail

    give(lambda q: found[q])

    @pl.when(jnp.sum(sum(bad)) > 0.0)
    def _():
        for q in range(groups):
            answers[q] = solve_again(work, full[q], rights[q])
        give(lambda q: answers[q])


def prepare_kernel(
    sets, owners, part, matrix, rhs, answers, solved, base, base_row, near, moves, fixed, leaf_moves, leaf_fixed
):
    size = matrix.shape[0]
    half = size // 2
    groups, _, n = answers.shape
    mine = unpack_symmetric(part[:half, :], part[half + 1 : half + 2, :])
    base[...] = matrix[...] + mine
    guess = matrix[...] + sets * mine
    near[...] = coarse_inverse(norm_bound(guess), [guess], ROOT_STEPS)[0]
    base_row[...] = jnp.broadcast_to(rhs[...] - part[half : half + 1, :], base_row.shape)
    for q in range(groups):
        fixed[q : q + 1, :] = answers[q, size : size + 1, :]
        moves[q] = answers[q, :size, :]
    for s in range(solved.shape[0]):
        owner = owners[s, :1, :1]
        own = jnp.zeros_like(answers[0])
        for q in range(groups):
            own = jnp.where(owner == q, answers[q], own)
        product = mul3(own, solved[s, :n, :])
        live = owner >= 0.0
        leaf_moves[s] = jnp.where(live, -product[:size], 0.0)
        last = solved[s, n : n + 8, :] - product[size : size + 8]
        leaf_fixed[s] = jnp.where(live, last, 0.0)


def root_kernel(
    sets, band, base, base_row, near, moves, fixed, leaf_moves, leaf_fixed, *refs
):
    others = refs[:-5]
    leaf_dir, node_dir, root_dir, full, work = refs[-5:]
    size = base.shape[0]
    half = size // 2
    groups, _, n = moves.shape
    system = base[...]
    right = base_row[...]
    for other in others:
        system = system + unpack_symmetric(other[:half, :], other[half + 1 : half + 2, :])
        right = right - other[half : half + 1, :]
    full[...] = system
    inverse = warm_inverse(system, near[...], 1.0 / sets, WARM_STEPS)
    found, bad = finish([system], [inverse], [right])

    def give(answer):
        root_dir[...] = answer
        column = jnp.broadcast_to(answer, (size, size)).T
        each = [jnp.sum(column * moves[q], axis=0, keepdims=True) for q in range(groups)]
        every = above(*each) + fixed[...]
        if band == n:
            node_dir[...] = every
        else:
            me = lax.axis_index("leaf")
            node_dir[...] = pltpu.roll(every, lax.rem(n - me * band, n), 1)[:, :band]
        wide = leaf_moves.shape[2] // size
        for s in range(leaf_moves.shape[0]):
            terms = beside(*[column] * wide) * leaf_moves[s]
            leaf_dir[s : s + 1, :] = jnp.sum(terms, axis=0, keepdims=True) + leaf_fixed[s, :1, :]

    give(found[0][:1])

    @pl.when(jnp.sum(bad[0]) > 0.0)
    def _():
        give(solve_again(work, full[...], right)[:1])


def gather_steps(extent):
    steps = []
    while extent > 1:
        extent //= 2
        steps.append(extent)
    return steps


def moved(values, axis, extent, distance):
    return lax.ppermute(values, axis, [(i, i ^ distance) for i in range(extent)])


def crossed(values, sets, distance):
    leaves = lax.axis_size("leaf")
    swap = 1 if leaves % 2 == 0 else 0
    pairs = [
        (i * sets + j, (i ^ swap) * sets + (j ^ distance)) for i in range(leaves) for j in range(sets)
    ]
    return lax.ppermute(values, ("leaf", "grp"), pairs)


def exchange(pieces, axis, extent, distance):
    sent = pieces[0] if len(pieces) == 1 else jnp.concatenate(pieces, axis=0)
    pieces.append(moved(sent, axis, extent, distance))


def doubled(values, axis, extent):
    pieces = [values]
    for distance in gather_steps(extent):
        exchange(pieces, axis, extent, distance)
    return pieces


def hold(pieces, value):
    pieces[-1] = lax.optimization_barrier((value, pieces[-1]))[1]


def source_offsets(steps):
    offsets = [0]
    for distance in steps:
        offsets = offsets + [o ^ distance for o in offsets]
    return tuple(offsets)


def other_parts(values, axis, extent):
    if extent == 1:
        return []
    if extent & (extent - 1):
        return [lax.psum(values, axis) - values]
    steps = gather_steps(extent)
    pieces = []
    for distance in reversed(steps):
        pieces.append(crossed(values, extent, distance))
        values = values + pieces[-1]
    return pieces


def remote(*values):
    return [pltpu.with_memory_space_constraint(v, pltpu.HBM) for v in values]


def local(*values):
    return [pltpu.with_memory_space_constraint(v, pltpu.VMEM) for v in values]


def body(
    leaves,
    sets,
    slot_parent,
    leaf_matrix,
    coupling,
    leaf_residual_rows,
    node_matrix,
    node_link,
    node_rhs,
    root_matrix,
    root_rhs,
):
    slots, n = leaf_residual_rows.shape
    groups, band, width = node_matrix.shape
    size = node_link.shape[2]
    doubling = leaves & (leaves - 1) == 0
    vmem = pl.BlockSpec(memory_space=pltpu.VMEM)
    smem = pl.BlockSpec(memory_space=pltpu.SMEM)
    params = pltpu.CompilerParams(vmem_limit_bytes=KERNEL_VMEM)

    paced = doubling and band % 8 == 0 and 4 <= leaves and 3 * band <= width
    hbm = pl.BlockSpec(memory_space=pltpu.HBM)
    nodes = [node_matrix, node_link, node_rhs]
    staged = [leaf_matrix, coupling, leaf_residual_rows, root_matrix, root_rhs[None, :]]
    owners, own, *near, root_matrix, root_row = pl.pallas_call(
        stage_kernel,
        out_shape=(
            pltpu.VMEM((slots, 8, width), f32),
            pltpu.VMEM((1, 2 * groups * band + groups, width), f32),
            *[pltpu.VMEM(a.shape, f32) for a in staged],
        ),
        in_specs=[smem] + [hbm] * (3 + len(staged)),
        out_specs=[vmem] * (2 + len(staged)),
        scratch_shapes=[pltpu.VMEM(a.shape, f32) for a in nodes]
        + [pltpu.SemaphoreType.DMA((3 + len(staged),))],
        compiler_params=params,
        name="stage",
    )(slot_parent, *remote(*nodes, *staged))
    def invert():
        return pl.pallas_call(
            invert_kernel,
            out_shape=pltpu.VMEM((slots, n, n), bf16),
            in_specs=[vmem],
            out_specs=vmem,
            compiler_params=params,
            cost_estimate=pl.CostEstimate(flops=COST, bytes_accessed=0, transcendentals=0),
            name="leaf_invert",
        )(*local(near[0]))

    def solve(matrix, coupling, residual, inverse):
        return pl.pallas_call(
            leaf_kernel,
            out_shape=(
                pltpu.VMEM((slots, width + 16, n), f32),
                pltpu.VMEM((slots, width // 2 + 8, width), f32),
            ),
            in_specs=[vmem] * 5,
            out_specs=(vmem, vmem),
            scratch_shapes=[
                pltpu.VMEM((n, n + 2 * width), f32),
            ],
            compiler_params=params,
            cost_estimate=pl.CostEstimate(flops=COST, bytes_accessed=0, transcendentals=0),
            name="leaf_solve",
        )(*local(owners, matrix, coupling, residual, inverse))

    if paced:
        steps = gather_steps(leaves)
        pair = [own]
        exchange(pair, "leaf", leaves, steps[0])
        inverse = invert()
        data = [
            pl.pallas_call(
                functools.partial(pack_kernel, leaves),
                out_shape=pltpu.VMEM((1, 3 * groups * band + groups, width), f32),
                in_specs=[vmem, vmem],
                out_specs=vmem,
                compiler_params=params,
                name="node_pack",
            )(*local(*pair))
        ]
        hold(data, inverse)
        exchange(data, "leaf", leaves, steps[1])
        solved, message = solve(*near, inverse)
        messages = [message]
        exchange(messages, "leaf", leaves, steps[-2])
        for step in steps[2:-1]:
            hold(data, messages[-1])
            exchange(data, "leaf", leaves, step)
        for step in steps[:-2]:
            exchange(messages, "leaf", leaves, step)
        hold(data, messages[-1])
        for pieces in (messages, data):
            exchange(pieces, "leaf", leaves, steps[-1])
        node_blocks = pl.pallas_call(
            functools.partial(assemble_kernel, leaves, source_offsets(steps[1:]), groups, band),
            out_shape=(
                pltpu.VMEM((groups, width // 2 + 8, width), f32),
                pltpu.VMEM((groups, width, size), f32),
            ),
            in_specs=[vmem] * len(data),
            out_specs=(vmem, vmem),
            compiler_params=params,
            name="node_assemble",
        )(*local(*data))
    else:
        rank = lax.axis_index("leaf")
        placed = lax.dynamic_update_slice(
            jnp.zeros((groups, width), f32), node_rhs, (jnp.zeros((), jnp.int32), rank * band)
        )
        every = lax.all_gather(
            jnp.concatenate([node_matrix, node_link], axis=0), "leaf", axis=1, tiled=True
        )
        blocks = every[:groups]
        half = width // 2
        row, col = grid_of(half, width)
        tops = jnp.where(col < row, jnp.roll(blocks[:, half:], half, 2), blocks[:, :half])
        shift = lax.psum(placed, "leaf")
        diagonal = jnp.where(
            jnp.arange(width) < half, 0.0, jnp.diagonal(blocks, axis1=1, axis2=2)
        )
        tails = jnp.stack([-shift, diagonal] + [jnp.zeros_like(shift)] * 6, axis=1)
        node_blocks = [jnp.concatenate([tops, tails], axis=1), every[groups:]]
        inverse = invert()
        solved, message = solve(*near, inverse)
        if doubling:
            messages = doubled(message, "leaf", leaves)
        else:
            messages = [lax.all_gather(message, "leaf", axis=0, tiled=True)]

    early = messages[:-1] or messages
    partial = pl.pallas_call(
        sum_kernel,
        out_shape=pltpu.VMEM((groups, width // 2 + 8, width), f32),
        in_specs=[vmem] * len(early),
        out_specs=vmem,
        compiler_params=params,
        cost_estimate=pl.CostEstimate(flops=COST // 4, bytes_accessed=0, transcendentals=0),
        name="node_sum",
    )(*local(*early))
    late = messages[len(early) :]

    answers, part = pl.pallas_call(
        node_kernel,
        out_shape=(
            pltpu.VMEM((groups, size + 16, width), f32),
            pltpu.VMEM((size // 2 + 8, size), f32),
        ),
        in_specs=[vmem] * (3 + len(late)),
        out_specs=(vmem, vmem),
        scratch_shapes=[
            pltpu.VMEM((groups, width, width), f32),
            pltpu.VMEM((groups, size + 16, width), f32),
            pltpu.VMEM((width, width + 2 * size), f32),
        ],
        compiler_params=params,
        name="node_solve",
    )(*local(*node_blocks, partial, *late))

    others = other_parts(part, "grp", sets)
    prepared = pl.pallas_call(
        functools.partial(prepare_kernel, sets),
        out_shape=(
            pltpu.VMEM((size, size), f32),
            pltpu.VMEM((16, size), f32),
            pltpu.VMEM((size, size), bf16),
            pltpu.VMEM((groups, size, width), f32),
            pltpu.VMEM((groups, width), f32),
            pltpu.VMEM((slots, size, n), f32),
            pltpu.VMEM((slots, 8, n), f32),
        ),
        in_specs=[vmem] * 6,
        out_specs=[vmem] * 7,
        compiler_params=params,
        cost_estimate=pl.CostEstimate(flops=COST // 2, bytes_accessed=0, transcendentals=0),
        name="root_prepare",
    )(*local(owners, part, root_matrix, root_row, answers, solved))

    leaf_dir, node_dir, root_dir = pl.pallas_call(
        functools.partial(root_kernel, sets, band),
        out_shape=(
            jax.ShapeDtypeStruct((slots, n), f32),
            jax.ShapeDtypeStruct((groups, band), f32),
            jax.ShapeDtypeStruct((1, size), f32),
        ),
        in_specs=[vmem] * (7 + len(others)),
        out_specs=(vmem, vmem, vmem),
        scratch_shapes=[
            pltpu.VMEM((size, size), f32),
            pltpu.VMEM((size, 2 * size), f32),
        ],
        compiler_params=params,
        name="root_solve",
    )(*local(*prepared, *others))
    return leaf_dir, node_dir, root_dir[0]


def solution(mesh):
    return jax.shard_map(
        functools.partial(body, mesh.shape["leaf"], mesh.shape["grp"]),
        mesh=mesh,
        in_specs=(
            P(("leaf", "grp")),
            P(("leaf", "grp"), None, None),
            P(("leaf", "grp"), None, None),
            P(("leaf", "grp"), None),
            P("grp", "leaf", None),
            P("grp", "leaf", None),
            P("grp", "leaf"),
            P(),
            P(),
        ),
        out_specs=(P(("leaf", "grp"), None), P("grp", "leaf"), P()),
        check_vma=False,
    )
```

```python
import functools

import jax
import jax.numpy as jnp
from jax import lax
from jax.experimental import pallas as pl
from jax.experimental.pallas import tpu as pltpu
from jax.sharding import PartitionSpec as P

f32 = jnp.float32
bf16 = jnp.bfloat16
FLOOR = 0.1
STEPS = 5
ROOT_STEPS = 6
WARM_STEPS = 3
COST = 3_000_000_000
KERNEL_VMEM = 24 << 20
ACCEPT = 4e-5


def mul(a, b):
    return jnp.dot(a, b, preferred_element_type=f32)


def split(a):
    high = a.astype(bf16)
    return high, (a - high.astype(f32)).astype(bf16)


def split3(a):
    high = a.astype(bf16)
    rest = a - high.astype(f32)
    mid = rest.astype(bf16)
    return high, mid, (rest - mid.astype(f32)).astype(bf16)


def beside(*parts):
    return jnp.concatenate(parts, axis=1)


def above(*parts):
    return jnp.concatenate(parts, axis=0)


def mul3(a, b):
    ah, al = split(a)
    bh, bl = split(b)
    return mul(beside(ah, ah, al), above(bh, bl, bh))


def grid_of(rows, cols):
    return (
        lax.broadcasted_iota(jnp.int32, (rows, cols), 0),
        lax.broadcasted_iota(jnp.int32, (rows, cols), 1),
    )


def identity(n):
    row, col = grid_of(n, n)
    return (row == col).astype(f32)


def pack_symmetric(full, extra):
    n = full.shape[0]
    half = n // 2
    row, col = grid_of(half, n)
    lower = full[half:]
    moved = pltpu.roll(lower, half, 1)
    top = jnp.where(col < row, moved, full[:half])
    diagonal = jnp.sum(jnp.where(col == row + half, lower, 0.0), axis=0, keepdims=True)
    row8, _ = grid_of(8, n)
    tail = jnp.where(row8 == 0, jnp.broadcast_to(extra, (8, n)), 0.0)
    tail = jnp.where(row8 == 1, jnp.broadcast_to(diagonal, (8, n)), tail)
    return top, tail


def unpack_symmetric(top, diagonal):
    half, n = top.shape
    row, col = grid_of(half, n)
    flipped = jnp.concatenate([top, jnp.zeros_like(top)], axis=0).T
    upper = jnp.where((col < half) & (col < row), flipped[:half], top)
    inner = pltpu.roll(jnp.where(col < row, top, flipped[:half]), half, 1)
    inner = jnp.where(col == row + half, jnp.broadcast_to(diagonal, (half, n)), inner)
    lower = jnp.where(col < half, flipped[half:], inner)
    return jnp.concatenate([upper, lower], axis=0)


def coarse_inverse(bound, matrices, steps):
    one = identity(matrices[0].shape[0])
    alpha = 2.0 / (bound + FLOOR)
    delta = (bound - FLOOR) / (bound + FLOOR)
    square = delta * delta
    scale = 2.0 / (2.0 - square)
    scaled = [alpha * m for m in matrices]
    errors = [(one - s).astype(bf16) for s in scaled]
    inverses = [((scale * alpha) * (2.0 * one - s)).astype(bf16) for s in scaled]
    errors = [(scale * (mul(e, e) - (0.5 * square) * one)).astype(bf16) for e in errors]
    n = one.shape[0]
    for left in reversed(range(steps - 1)):
        delta = square / (2.0 - square)
        square = delta * delta
        scale = 2.0 / (2.0 - square)
        if left:
            both = [mul(e, beside(e, v)) for e, v in zip(errors, inverses)]
            errors = [(scale * (b[:, :n] - (0.5 * square) * one)).astype(bf16) for b in both]
            news = [b[:, n:] for b in both]
        else:
            news = [mul(e, v) for e, v in zip(errors, inverses)]
        inverses = [(scale * (v.astype(f32) + b)).astype(bf16) for v, b in zip(inverses, news)]
    return inverses


def warm_inverse(matrix, near, low, steps):
    one = identity(matrix.shape[0])
    product = mul(near, matrix.astype(bf16))
    bound = jnp.maximum(norm_bound(product), 2.0 * low)
    alpha = 2.0 / (bound + low)
    delta = (bound - low) / (bound + low)
    square = delta * delta
    scale = 2.0 / (2.0 - square)
    error = (one - alpha * product).astype(bf16)
    inverse = (alpha * near.astype(f32)).astype(bf16)
    for step in range(steps):
        inverse = (scale * (inverse.astype(f32) + mul(error, inverse))).astype(bf16)
        if step + 1 < steps:
            error = (scale * (mul(error, error) - (0.5 * square) * one)).astype(bf16)
            delta = square / (2.0 - square)
            square = delta * delta
            scale = 2.0 / (2.0 - square)
    return inverse


def finish(matrices, inverses, rights):
    errors = [
        identity(m.shape[0]) - mul(beside(v, v), above(*split(m)))
        for m, v in zip(matrices, inverses)
    ]
    pieces = [split(e) for e in errors]
    squares = [mul(h, h).astype(bf16) for h, _ in pieces]
    first = []
    for right, (eh, el) in zip(rights, pieces):
        rh, rl = split(right)
        first.append(right + mul(beside(rh, rh, rl), above(eh, el, eh)))
    second = [mul(z.astype(bf16), s) for z, s in zip(first, squares)]
    found = [
        mul(beside(*split(z + d)), above(v, v)) for z, d, v in zip(first, second, inverses)
    ]
    return found, [misfits(d, z) for z, d in zip(first, second)]


def misfits(change, values):
    got = jnp.sum(change * change, axis=1, keepdims=True)
    allowed = ACCEPT * jnp.sum(values * values, axis=1, keepdims=True)
    return jnp.where(got <= allowed, 0.0, 1.0)


def eliminate(work):
    n, width = work.shape

    def step(k, carry):
        row, col = grid_of(8, width)
        base = pl.multiple_of((k // 8) * 8, 8)
        block = work[pl.ds(base, 8), :]
        pivot_row = jnp.sum(jnp.where(row == k - base, block, 0.0), axis=0, keepdims=True)
        pivot = jnp.sum(jnp.where(col[:1] == k, pivot_row, 0.0), axis=1, keepdims=True)
        scaled = pivot_row / pivot
        full = work[...]
        row, col = grid_of(n, width)
        column = jnp.sum(jnp.where(col == k, full, 0.0), axis=1, keepdims=True)
        work[...] = jnp.where(row == k, scaled, full - column * scaled)
        return carry

    lax.fori_loop(0, n, step, 0)


def solve_again(work, matrix, right):
    n, rows = matrix.shape[0], right.shape[0]
    work[:, :n] = matrix
    padded = above(right, jnp.zeros((work.shape[1] - n - rows, n), f32))
    work[:, n:] = padded.T
    eliminate(work)
    return work[:, n:].T[:rows]


def norm_bound(*matrices):
    sums = [jnp.sum(jnp.abs(m), axis=0, keepdims=True) for m in matrices]
    most = sums[0]
    for other in sums[1:]:
        most = jnp.maximum(most, other)
    return jnp.max(most, axis=1, keepdims=True)


def stage_kernel(parent, matrix, link, rhs, *refs):
    matrix_rows, link_rows, rhs_rows, sems = refs[-4:]
    count = (len(refs) - 6) // 2
    rest, owners, own, targets = refs[:count], refs[count], refs[count + 1], refs[count + 2 : -4]
    pairs = ((matrix, matrix_rows), (link, link_rows), (rhs, rhs_rows), *zip(rest, targets))
    copies = [
        pltpu.make_async_copy(source, target, sems.at[i])
        for i, (source, target) in enumerate(pairs)
    ]
    for copy in copies:
        copy.start()
    for s in range(owners.shape[0]):
        owners[s] = jnp.full(owners.shape[1:], parent[s].astype(f32))
    groups, band, _ = matrix_rows.shape
    rows = groups * band
    own[0, 2 * rows :, :] = jnp.zeros((groups, own.shape[2]), f32)
    for copy in copies[:3]:
        copy.wait()
    for q in range(groups):
        own[0, q * band : (q + 1) * band, :] = matrix_rows[q]
        own[0, rows + q * band : rows + (q + 1) * band, :] = link_rows[q]
    own[0, 2 * rows :, :band] = rhs_rows[...]
    for copy in copies[3:]:
        copy.wait()


def invert_kernel(matrix, inverse):
    for s in range(matrix.shape[0]):
        block = matrix[s]
        inverse[s] = coarse_inverse(norm_bound(block), [block], STEPS)[0]


def leaf_kernel(owners, matrix, coupling, residual, inverse, solved, message, work):
    n = matrix.shape[1]
    width = coupling.shape[2]
    for s in range(matrix.shape[0]):

        def right_side():
            return above(coupling[s].T, jnp.broadcast_to(residual[s : s + 1, :], (16, n)))

        def give(found):
            solved[s] = found
            product = mul3(found, coupling[s])
            top, tail = pack_symmetric(product[:width], product[width : width + 1])
            row8, _ = grid_of(8, width)
            message[s, : width // 2, :] = top
            message[s, width // 2 :, :] = jnp.where(row8 == 2, owners[s], tail)

        found, bad = finish([matrix[s]], [inverse[s]], [right_side()])
        give(found[0])

        @pl.when(jnp.sum(bad[0]) > 0.0)
        def _():
            give(solve_again(work, matrix[s], right_side()))


def pack_kernel(leaves, own, other, packed):
    n = own.shape[2]
    half = n // 2
    band = half // (leaves // 2)
    groups = own.shape[1] // (2 * band + 1)
    rows = groups * band
    here = lax.axis_index("leaf")
    is_top = here < leaves // 2
    place = lax.rem(here, leaves // 2) * band
    top = jnp.where(is_top, own[0], other[0])
    low = jnp.where(is_top, other[0], own[0])
    row, col = grid_of(band, n)
    row = row + place
    diagonals = []
    for q in range(groups):
        at = slice(q * band, (q + 1) * band)
        packed[0, at, :] = jnp.where(col < row, pltpu.roll(low[at], half, 1), top[at])
        diagonals.append(
            jnp.sum(jnp.where(col == row + half, low[at], 0.0), axis=0, keepdims=True)
        )
    packed[0, rows : 2 * rows, :] = top[rows : 2 * rows]
    packed[0, 2 * rows : 3 * rows, :] = low[rows : 2 * rows]
    _, col = grid_of(groups, n)
    diagonal = pltpu.roll(above(*diagonals), lax.rem(half + 2 * band - place, n), 1)
    last = jnp.where(col < 2 * band, pltpu.roll(low[2 * rows :], band, 1), diagonal)
    last = jnp.where(col < band, top[2 * rows :], last)
    packed[0, 3 * rows :, :] = jnp.where(col < 3 * band, last, 0.0)


def assemble_kernel(leaves, sources, groups, band, *refs):
    data = refs[:-2]
    regular, links = refs[-2:]
    n = regular.shape[2]
    half = n // 2
    rows = groups * band
    here = lax.axis_index("leaf")
    row, col = grid_of(groups, n)
    at = 0
    shift = jnp.zeros((groups, n), f32)
    diagonal = jnp.zeros((groups, n), f32)
    for piece in data:
        for j in range(piece.shape[0]):
            place = lax.rem(here ^ sources[at], leaves // 2) * band
            place = pl.multiple_of(place, band)
            at += 1
            for q in range(groups):
                regular[q, pl.ds(place, band), :] = piece[j, q * band : (q + 1) * band, :]
                start = rows + q * band
                links[q, pl.ds(place, band), :] = piece[j, start : start + band, :]
                start = start + rows
                links[q, pl.ds(half + place, band), :] = piece[j, start : start + band, :]
            last = piece[j, 3 * rows :, :]
            first = jnp.where(col < band, last, 0.0)
            second = jnp.where((col >= band) & (col < 2 * band), last, 0.0)
            third = jnp.where(col >= 2 * band, last, 0.0)
            shift = shift + pltpu.roll(first, place, 1)
            shift = shift + pltpu.roll(second, lax.rem(half + place - band + n, n), 1)
            diagonal = diagonal + pltpu.roll(third, lax.rem(half + place - 2 * band + n, n), 1)
    row8, _ = grid_of(8, n)
    for q in range(groups):
        tail = jnp.where(row8 == 0, -shift[q : q + 1], 0.0)
        regular[q, half:, :] = jnp.where(row8 == 1, diagonal[q : q + 1], tail)


def add_messages(sums, messages):
    if not messages:
        return sums
    row = messages[0].shape[1] - 6
    for piece in messages:
        for j in range(piece.shape[0]):
            message = piece[j]
            owner = message[row : row + 1, :]
            sums = [x + jnp.where(owner == q, message, 0.0) for q, x in enumerate(sums)]
    return sums


def sum_kernel(*refs):
    sums = refs[-1]
    groups = sums.shape[0]
    zero = jnp.zeros(sums.shape[1:], f32)
    for q, total in enumerate(add_messages([zero] * groups, refs[:-1])):
        sums[q] = total


def node_kernel(regular, links, partial, *refs):
    messages = refs[:-5]
    answers, message, full, rights, work = refs[-5:]
    groups, n, width = links.shape
    half = n // 2
    sums = add_messages([regular[q] + partial[q] for q in range(groups)], messages)
    tops = [x[:half] for x in sums]
    tails = [x[half:] for x in sums]
    for q in range(groups):
        full[q] = unpack_symmetric(tops[q], tails[q][1:2])
        rights[q, :width] = links[q].T
        rights[q, width:] = jnp.broadcast_to(tails[q][:1], (16, n))
    blocks = [full[q] for q in range(groups)]
    inverses = coarse_inverse(norm_bound(*blocks), blocks, STEPS)
    found, bad = finish(blocks, inverses, [rights[q] for q in range(groups)])

    def give(found):
        lefts, rights_ = [], []
        for q in range(groups):
            answers[q] = found(q)
            ah, al = split(found(q))
            bh, bl = split(links[q])
            lefts += [ah, ah, al]
            rights_ += [bh, bl, bh]
        total = mul(beside(*lefts), above(*rights_))
        top, tail = pack_symmetric(total[:width], total[width : width + 1])
        message[: width // 2, :] = top
        message[width // 2 :, :] = tail

    give(lambda q: found[q])

    @pl.when(jnp.sum(sum(bad)) > 0.0)
    def _():
        for q in range(groups):
            answers[q] = solve_again(work, full[q], rights[q])
        give(lambda q: answers[q])


def prepare_kernel(
    sets, owners, part, matrix, rhs, answers, solved, base, base_row, near, moves, fixed, leaf_moves, leaf_fixed
):
    size = matrix.shape[0]
    half = size // 2
    groups, _, n = answers.shape
    mine = unpack_symmetric(part[:half, :], part[half + 1 : half + 2, :])
    base[...] = matrix[...] + mine
    guess = matrix[...] + sets * mine
    near[...] = coarse_inverse(norm_bound(guess), [guess], ROOT_STEPS)[0]
    base_row[...] = jnp.broadcast_to(rhs[...] - part[half : half + 1, :], base_row.shape)
    for q in range(groups):
        fixed[q : q + 1, :] = answers[q, size : size + 1, :]
        moves[q] = answers[q, :size, :]
    for s in range(solved.shape[0]):
        owner = owners[s, :1, :1]
        own = jnp.zeros_like(answers[0])
        for q in range(groups):
            own = jnp.where(owner == q, answers[q], own)
        product = mul3(own, solved[s, :n, :])
        live = owner >= 0.0
        leaf_moves[s] = jnp.where(live, -product[:size], 0.0)
        last = solved[s, n : n + 8, :] - product[size : size + 8]
        leaf_fixed[s] = jnp.where(live, last, 0.0)


def root_kernel(
    sets, band, base, base_row, near, moves, fixed, leaf_moves, leaf_fixed, *refs
):
    others = refs[:-5]
    leaf_dir, node_dir, root_dir, full, work = refs[-5:]
    size = base.shape[0]
    half = size // 2
    groups, _, n = moves.shape
    system = base[...]
    right = base_row[...]
    for other in others:
        system = system + unpack_symmetric(other[:half, :], other[half + 1 : half + 2, :])
        right = right - other[half : half + 1, :]
    full[...] = system
    inverse = warm_inverse(system, near[...], 1.0 / sets, WARM_STEPS)
    found, bad = finish([system], [inverse], [right])

    def give(answer):
        root_dir[...] = answer
        column = jnp.broadcast_to(answer, (size, size)).T
        each = [jnp.sum(column * moves[q], axis=0, keepdims=True) for q in range(groups)]
        every = above(*each) + fixed[...]
        if band == n:
            node_dir[...] = every
        else:
            me = lax.axis_index("leaf")
            node_dir[...] = pltpu.roll(every, lax.rem(n - me * band, n), 1)[:, :band]
        wide = leaf_moves.shape[2] // size
        for s in range(leaf_moves.shape[0]):
            terms = beside(*[column] * wide) * leaf_moves[s]
            leaf_dir[s : s + 1, :] = jnp.sum(terms, axis=0, keepdims=True) + leaf_fixed[s, :1, :]

    give(found[0][:1])

    @pl.when(jnp.sum(bad[0]) > 0.0)
    def _():
        give(solve_again(work, full[...], right)[:1])


def gather_steps(extent):
    steps = []
    while extent > 1:
        extent //= 2
        steps.append(extent)
    return steps


def moved(values, axis, extent, distance):
    return lax.ppermute(values, axis, [(i, i ^ distance) for i in range(extent)])


def crossed(values, sets, distance):
    leaves = lax.axis_size("leaf")
    swap = 1 if leaves % 2 == 0 else 0
    pairs = [
        (i * sets + j, (i ^ swap) * sets + (j ^ distance)) for i in range(leaves) for j in range(sets)
    ]
    return lax.ppermute(values, ("leaf", "grp"), pairs)


def exchange(pieces, axis, extent, distance):
    sent = pieces[0] if len(pieces) == 1 else jnp.concatenate(pieces, axis=0)
    pieces.append(moved(sent, axis, extent, distance))


def doubled(values, axis, extent):
    pieces = [values]
    for distance in gather_steps(extent):
        exchange(pieces, axis, extent, distance)
    return pieces


def hold(pieces, value):
    pieces[-1] = lax.optimization_barrier((value, pieces[-1]))[1]


def source_offsets(steps):
    offsets = [0]
    for distance in steps:
        offsets = offsets + [o ^ distance for o in offsets]
    return tuple(offsets)


def other_parts(values, axis, extent):
    if extent == 1:
        return []
    if extent & (extent - 1):
        return [lax.psum(values, axis) - values]
    steps = gather_steps(extent)
    pieces = []
    for distance in reversed(steps):
        pieces.append(crossed(values, extent, distance))
        values = values + pieces[-1]
    return pieces


def remote(*values):
    return [pltpu.with_memory_space_constraint(v, pltpu.HBM) for v in values]


def local(*values):
    return [pltpu.with_memory_space_constraint(v, pltpu.VMEM) for v in values]


def body(
    leaves,
    sets,
    slot_parent,
    leaf_matrix,
    coupling,
    leaf_residual_rows,
    node_matrix,
    node_link,
    node_rhs,
    root_matrix,
    root_rhs,
):
    slots, n = leaf_residual_rows.shape
    groups, band, width = node_matrix.shape
    size = node_link.shape[2]
    doubling = leaves & (leaves - 1) == 0
    vmem = pl.BlockSpec(memory_space=pltpu.VMEM)
    smem = pl.BlockSpec(memory_space=pltpu.SMEM)
    params = pltpu.CompilerParams(vmem_limit_bytes=KERNEL_VMEM)

    paced = doubling and band % 8 == 0 and 4 <= leaves and 3 * band <= width
    hbm = pl.BlockSpec(memory_space=pltpu.HBM)
    nodes = [node_matrix, node_link, node_rhs]
    staged = [leaf_matrix, coupling, leaf_residual_rows, root_matrix, root_rhs[None, :]]
    owners, own, *near, root_matrix, root_row = pl.pallas_call(
        stage_kernel,
        out_shape=(
            pltpu.VMEM((slots, 8, width), f32),
            pltpu.VMEM((1, 2 * groups * band + groups, width), f32),
            *[pltpu.VMEM(a.shape, f32) for a in staged],
        ),
        in_specs=[smem] + [hbm] * (3 + len(staged)),
        out_specs=[vmem] * (2 + len(staged)),
        scratch_shapes=[pltpu.VMEM(a.shape, f32) for a in nodes]
        + [pltpu.SemaphoreType.DMA((3 + len(staged),))],
        compiler_params=params,
        name="stage",
    )(slot_parent, *remote(*nodes, *staged))
    def invert():
        return pl.pallas_call(
            invert_kernel,
            out_shape=pltpu.VMEM((slots, n, n), bf16),
            in_specs=[vmem],
            out_specs=vmem,
            compiler_params=params,
            cost_estimate=pl.CostEstimate(flops=COST, bytes_accessed=0, transcendentals=0),
            name="leaf_invert",
        )(*local(near[0]))

    def solve(matrix, coupling, residual, inverse):
        return pl.pallas_call(
            leaf_kernel,
            out_shape=(
                pltpu.VMEM((slots, width + 16, n), f32),
                pltpu.VMEM((slots, width // 2 + 8, width), f32),
            ),
            in_specs=[vmem] * 5,
            out_specs=(vmem, vmem),
            scratch_shapes=[
                pltpu.VMEM((n, n + 2 * width), f32),
            ],
            compiler_params=params,
            cost_estimate=pl.CostEstimate(flops=COST, bytes_accessed=0, transcendentals=0),
            name="leaf_solve",
        )(*local(owners, matrix, coupling, residual, inverse))

    if paced:
        steps = gather_steps(leaves)
        pair = [own]
        exchange(pair, "leaf", leaves, steps[0])
        inverse = invert()
        data = [
            pl.pallas_call(
                functools.partial(pack_kernel, leaves),
                out_shape=pltpu.VMEM((1, 3 * groups * band + groups, width), f32),
                in_specs=[vmem, vmem],
                out_specs=vmem,
                compiler_params=params,
                name="node_pack",
            )(*local(*pair))
        ]
        hold(data, inverse)
        exchange(data, "leaf", leaves, steps[1])
        solved, message = solve(*near, inverse)
        messages = [message]
        exchange(messages, "leaf", leaves, steps[-2])
        for step in steps[2:-1]:
            hold(data, messages[-1])
            exchange(data, "leaf", leaves, step)
        for step in steps[:-2]:
            exchange(messages, "leaf", leaves, step)
        hold(data, messages[-1])
        for pieces in (messages, data):
            exchange(pieces, "leaf", leaves, steps[-1])
        node_blocks = pl.pallas_call(
            functools.partial(assemble_kernel, leaves, source_offsets(steps[1:]), groups, band),
            out_shape=(
                pltpu.VMEM((groups, width // 2 + 8, width), f32),
                pltpu.VMEM((groups, width, size), f32),
            ),
            in_specs=[vmem] * len(data),
            out_specs=(vmem, vmem),
            compiler_params=params,
            name="node_assemble",
        )(*local(*data))
    else:
        rank = lax.axis_index("leaf")
        placed = lax.dynamic_update_slice(
            jnp.zeros((groups, width), f32), node_rhs, (jnp.zeros((), jnp.int32), rank * band)
        )
        every = lax.all_gather(
            jnp.concatenate([node_matrix, node_link], axis=0), "leaf", axis=1, tiled=True
        )
        blocks = every[:groups]
        half = width // 2
        row, col = grid_of(half, width)
        tops = jnp.where(col < row, jnp.roll(blocks[:, half:], half, 2), blocks[:, :half])
        shift = lax.psum(placed, "leaf")
        diagonal = jnp.where(
            jnp.arange(width) < half, 0.0, jnp.diagonal(blocks, axis1=1, axis2=2)
        )
        tails = jnp.stack([-shift, diagonal] + [jnp.zeros_like(shift)] * 6, axis=1)
        node_blocks = [jnp.concatenate([tops, tails], axis=1), every[groups:]]
        inverse = invert()
        solved, message = solve(*near, inverse)
        if doubling:
            messages = doubled(message, "leaf", leaves)
        else:
            messages = [lax.all_gather(message, "leaf", axis=0, tiled=True)]

    early = messages[:-1] or messages
    partial = pl.pallas_call(
        sum_kernel,
        out_shape=pltpu.VMEM((groups, width // 2 + 8, width), f32),
        in_specs=[vmem] * len(early),
        out_specs=vmem,
        compiler_params=params,
        cost_estimate=pl.CostEstimate(flops=COST // 4, bytes_accessed=0, transcendentals=0),
        name="node_sum",
    )(*local(*early))
    late = messages[len(early) :]

    answers, part = pl.pallas_call(
        node_kernel,
        out_shape=(
            pltpu.VMEM((groups, size + 16, width), f32),
            pltpu.VMEM((size // 2 + 8, size), f32),
        ),
        in_specs=[vmem] * (3 + len(late)),
        out_specs=(vmem, vmem),
        scratch_shapes=[
            pltpu.VMEM((groups, width, width), f32),
            pltpu.VMEM((groups, size + 16, width), f32),
            pltpu.VMEM((width, width + 2 * size), f32),
        ],
        compiler_params=params,
        name="node_solve",
    )(*local(*node_blocks, partial, *late))

    others = other_parts(part, "grp", sets)
    prepared = pl.pallas_call(
        functools.partial(prepare_kernel, sets),
        out_shape=(
            pltpu.VMEM((size, size), f32),
            pltpu.VMEM((16, size), f32),
            pltpu.VMEM((size, size), bf16),
            pltpu.VMEM((groups, size, width), f32),
            pltpu.VMEM((groups, width), f32),
            pltpu.VMEM((slots, size, n), f32),
            pltpu.VMEM((slots, 8, n), f32),
        ),
        in_specs=[vmem] * 6,
        out_specs=[vmem] * 7,
        compiler_params=params,
        cost_estimate=pl.CostEstimate(flops=COST // 2, bytes_accessed=0, transcendentals=0),
        name="root_prepare",
    )(*local(owners, part, root_matrix, root_row, answers, solved))

    leaf_dir, node_dir, root_dir = pl.pallas_call(
        functools.partial(root_kernel, sets, band),
        out_shape=(
            jax.ShapeDtypeStruct((slots, n), f32),
            jax.ShapeDtypeStruct((groups, band), f32),
            jax.ShapeDtypeStruct((1, size), f32),
        ),
        in_specs=[vmem] * (7 + len(others)),
        out_specs=(vmem, vmem, vmem),
        scratch_shapes=[
            pltpu.VMEM((size, size), f32),
            pltpu.VMEM((size, 2 * size), f32),
        ],
        compiler_params=params,
        name="root_solve",
    )(*local(*prepared, *others))
    return leaf_dir, node_dir, root_dir[0]


def solution(mesh):
    return jax.shard_map(
        functools.partial(body, mesh.shape["leaf"], mesh.shape["grp"]),
        mesh=mesh,
        in_specs=(
            P(("leaf", "grp")),
            P(("leaf", "grp"), None, None),
            P(("leaf", "grp"), None, None),
            P(("leaf", "grp"), None),
            P("grp", "leaf", None),
            P("grp", "leaf", None),
            P("grp", "leaf"),
            P(),
            P(),
        ),
        out_specs=(P(("leaf", "grp"), None), P("grp", "leaf"), P()),
        check_vma=False,
    )
```
